32 devices in a mesh: sec: 8 (over y, x, core), strip: 4 (over z).
Axes of the slice: x: 2, y: 2, z: 4, core: 2. Of those that a mesh axis runs over, the one named last changes fastest.
Arguments:
- images: bfloat16 [8, 512, 1024], P('sec', 'strip'), may hold values from -6 to 6
- row_weights: float32 [8, 4, 512], P('sec', None, 'strip'), may hold values from 0.05 to 0.5
- row_shift: int32 [8, 4], P('sec', 'strip'), may hold values from -4 to 4
- col_weights: bfloat16 [8, 4, 1024], P('sec'), may hold values from 0.049804688 to 0.5
- col_shift: int32 [8], P('sec'), may hold values from -32 to 32
- pair_on: int32 [8, 3], replicated, may hold values 0 or 1
Outputs:
- grad_warped: float32 [8, 512, 1024], P('sec', 'strip')
- displacement: float32 [2, 8, 512, 1024], P(None, 'sec', 'strip')
The draws below stay inside these ranges and needn't reach their ends.
All inputs are finite; a program needn't handle non-finite values.
Results may differ from the reference program's by a relative error of at most 0.0047.
Values may be sent and summed in bfloat16 or wider, within the bound.
A program may use at most 64 MiB of HBM per device.

```python
import jax
import jax.numpy as jnp
from jax import lax

ROWS_DEV = 128
WIDTH = 1024
TAP_COUNT = 4
MAX_SHIFT = 4
COL_REACH = 32
RADIUS = 4
PAIR_REACH = 3
SECTIONS = 8
HEIGHT = 512
STRIPS = 4


def with_ends(result, own_key, smallest, top_value):
    longest = result.shape.index(max(result.shape))
    spots = []
    for shift in (0, 1):
        where = [jax.random.randint(jax.random.fold_in(own_key, axis), (), 0, length) for axis, length in enumerate(result.shape)]
        where[longest] = (where[longest] + shift) % result.shape[longest]
        spots.append(tuple(where))
    return result.at[spots[0]].set(smallest).at[spots[1]].set(top_value)


def level_of(key, extent, split, low, high):
    def one(axis_at, blocks):
        steps = jax.random.uniform(jax.random.fold_in(jax.random.fold_in(key, 6), axis_at), (blocks,), jnp.float32, low / len(split), high / len(split))
        return jnp.repeat(jnp.exp(steps), extent[axis_at] // blocks).reshape((-1,) + (1,) * (len(extent) - axis_at - 1))

    level = one(*split[0])
    for cut in split[1:]:
        level = level * one(*cut)
    return level


def normal_values(rng, dims, deviation, limit, cuts=(), kind=jnp.bfloat16):
    entries = jax.random.normal(rng, dims, jnp.float32) * deviation
    if len(cuts) > 0:
        entries = level_of(rng, dims, cuts, -0.22, 0.18) * entries
    return jnp.clip(entries, min=-limit, max=limit).astype(kind)


def setup_inputs(seed: int = 0) -> dict:
    key_list = jax.random.split(jax.random.key(seed), 7)
    return {
        "images": normal_values(key_list[0], (SECTIONS, HEIGHT, WIDTH), 1.0, 6.0, ((0, 8), (1, 4))),
        "row_weights": jnp.clip(0.05 + 0.45 * jax.random.uniform(key_list[1], (SECTIONS, TAP_COUNT, HEIGHT), jnp.float32) ** level_of(key_list[1], (SECTIONS, TAP_COUNT, HEIGHT), ((0, 8), (2, 4)), -0.2, 0.2), 0.05, 0.5),
        "row_shift": with_ends(jax.random.randint(key_list[2], (SECTIONS, STRIPS), 0 - MAX_SHIFT, MAX_SHIFT + 1), jax.random.fold_in(key_list[2], 1), 0 - MAX_SHIFT, MAX_SHIFT).astype(jnp.int32),
        "col_weights": jnp.clip(0.049804688 + 0.4501953 * jax.random.uniform(key_list[3], (SECTIONS, TAP_COUNT, WIDTH), jnp.float32) ** level_of(key_list[3], (SECTIONS, TAP_COUNT, WIDTH), ((0, 8),), -0.2, 0.2), 0.049804688, 0.5).astype(jnp.bfloat16),
        "col_shift": with_ends(jax.random.randint(key_list[4], (SECTIONS,), 0 - COL_REACH, COL_REACH + 1), jax.random.fold_in(key_list[4], 1), 0 - COL_REACH, COL_REACH).astype(jnp.int32),
        "pair_on": with_ends((jax.random.randint(key_list[5], (SECTIONS, PAIR_REACH), 0, 4) < 3).astype(jnp.int32), jax.random.fold_in(key_list[5], 1), 0, 1),
    }


variance_bias = 0.25

def box_sum(field):
    size_box = 2 * RADIUS + 1
    row_count = field.shape[-2]
    col_count = field.shape[-1]
    widths = [(0, 0)] * (field.ndim - 2) + [(RADIUS, RADIUS), (RADIUS, RADIUS)]
    padded = jnp.pad(field, widths)
    across = padded[..., 0:row_count, :]
    for step_row in range(1, size_box):
        across = across + padded[..., step_row:step_row + row_count, :]
    running = across[..., 0:col_count]
    for step_col in range(1, size_box):
        running = running + across[..., step_col:step_col + col_count]
    return running

def warp_section(section_items):
    image, weights, shifts, column_taps, column_shift = section_items
    source_depth = MAX_SHIFT + 2
    padded = jnp.pad(image, ((source_depth, source_depth), (0, 0)))
    shift_rows = jnp.repeat(shifts.astype(jnp.int32), ROWS_DEV)
    base_rows = jnp.arange(HEIGHT, dtype=jnp.int32) + shift_rows + (source_depth - 1)
    running = jnp.zeros((HEIGHT, WIDTH), jnp.float32)
    for tap_index in range(TAP_COUNT):
        taken = jnp.take(padded, (base_rows + tap_index).astype(jnp.int32), axis=0)
        running = running + weights[tap_index][:, None].astype(jnp.float32) * taken.astype(jnp.float32)
    row_warped = running.astype(jnp.bfloat16)
    row_ids = lax.broadcasted_iota(jnp.int32, (WIDTH, WIDTH), 0)
    col_ids = lax.broadcasted_iota(jnp.int32, (WIDTH, WIDTH), 1)
    offsets = row_ids - col_ids - column_shift.astype(jnp.int32) + 1
    matrix = jnp.zeros((WIDTH, WIDTH), column_taps.dtype)
    for tap_index in range(TAP_COUNT):
        matrix = jnp.where(offsets == tap_index, column_taps[tap_index][None, :], matrix)
    return jnp.dot(row_warped, matrix, preferred_element_type=jnp.float32).astype(jnp.bfloat16)

def pair_grads(left_field, right_field, weight):
    box_cells = float((2 * RADIUS + 1) ** 2)
    mean_left = box_sum(left_field) / box_cells
    mean_right = box_sum(right_field) / box_cells
    var_left = box_sum(left_field * left_field) / box_cells - mean_left * mean_left + variance_bias
    var_right = box_sum(right_field * right_field) / box_cells - mean_right * mean_right + variance_bias
    covariance = box_sum(left_field * right_field) / box_cells - mean_left * mean_right
    denom_root = jnp.sqrt(var_left * var_right)
    ncc_value = covariance / denom_root
    g_cov = -weight / denom_root
    g_left = weight * ncc_value / (2.0 * var_left)
    g_right = weight * ncc_value / (2.0 * var_right)
    h_left = -g_cov * mean_right - 2.0 * g_left * mean_left
    h_right = -g_cov * mean_left - 2.0 * g_right * mean_right
    boxed_cov = box_sum(g_cov)
    grad_left = (box_sum(h_left) + 2.0 * left_field * box_sum(g_left) + right_field * boxed_cov) / box_cells
    grad_right = (box_sum(h_right) + 2.0 * right_field * box_sum(g_right) + left_field * boxed_cov) / box_cells
    return (grad_left, grad_right)

def displace(section_items):
    field, grads = section_items
    field_wide = field.astype(jnp.float32)
    rows_padded = jnp.pad(field_wide, ((1, 1), (0, 0)))
    slope_rows = (rows_padded[2:] - rows_padded[:-2]) * 0.5
    cols_padded = jnp.pad(field_wide, ((0, 0), (1, 1)))
    slope_cols = (cols_padded[:, 2:] - cols_padded[:, :-2]) * 0.5
    products = jnp.stack([grads * slope_rows, grads * slope_cols])
    return -box_sum(products) / 9.0

def reference(images, row_weights, row_shift, col_weights, col_shift, pair_on):
    warped = lax.map(warp_section, (images, row_weights, row_shift, col_weights, col_shift))
    grads = jnp.zeros((SECTIONS, HEIGHT, WIDTH), jnp.float32)
    for distance in range(1, PAIR_REACH + 1):
        pair_count = SECTIONS - distance

        def one_pair(pair_items):
            left_img, right_img, weight = pair_items
            return pair_grads(left_img.astype(jnp.float32), right_img.astype(jnp.float32), weight)
        grad_left, grad_right = lax.map(one_pair, (warped[:pair_count], warped[distance:], pair_on[:pair_count, distance - 1].astype(jnp.float32)))
        grads = grads.at[:pair_count].add(grad_left)
        grads = grads.at[distance:].add(grad_right)
    displacement = lax.map(displace, (warped, grads))
    return (grads, jnp.transpose(displacement, (1, 0, 2, 3)))
```

```python
import functools

import jax
import jax.numpy as jnp
from jax import lax
from jax.experimental import pallas as pl
from jax.experimental.pallas import tpu as pltpu
from jax.sharding import PartitionSpec as P

TAP_COUNT = 4
MAX_SHIFT = 4
RADIUS = 4
PAIR_REACH = 3


variance_bias = 0.25


def padded_2(block, sides, width):
    for axis, dim in sides:
        count = lax.axis_size(axis)
        forward = [(i, i + 1) for i in range(count - 1)]
        backward = [(target, source) for source, target in forward]
        low = lax.ppermute(
            lax.slice_in_dim(block, block.shape[dim] - width, None, axis=dim), axis, forward
        )
        high = lax.ppermute(lax.slice_in_dim(block, 0, width, axis=dim), axis, backward)
        block = jnp.concatenate([low, block, high], axis=dim)
    return block


def passed_along(value, axis, steps):
    count = lax.axis_size(axis)
    initial, last = (max(0, -steps), min(count, count - steps))
    return lax.ppermute(value, axis, [(source, source + steps) for source in range(initial, last)])


def box_rows(field, out_rows):
    running = field[..., 0:out_rows, :]
    for step_row in range(1, 2 * RADIUS + 1):
        running = running + field[..., step_row : step_row + out_rows, :]
    return running


def box_cols(field):
    col_count = field.shape[-1]
    widths = [(0, 0)] * (field.ndim - 1) + [(RADIUS, RADIUS)]
    padded = jnp.pad(field, widths)
    running = padded[..., 0:col_count]
    for step_col in range(1, 2 * RADIUS + 1):
        running = running + padded[..., step_col : step_col + col_count]
    return running


def box_sum(field, out_rows):
    return box_cols(box_rows(field, out_rows))


def pair_grads(left_rim, right_rim, weight, depth, row_count):
    box_cells = float((2 * RADIUS + 1) ** 2)
    left_field = left_rim.astype(jnp.float32)
    right_field = right_rim.astype(jnp.float32)
    mean_left = box_sum(left_field, row_count) / box_cells
    mean_right = box_sum(right_field, row_count) / box_cells
    var_left = (
        box_sum(left_field * left_field, row_count) / box_cells
        - mean_left * mean_left
        + variance_bias
    )
    var_right = (
        box_sum(right_field * right_field, row_count) / box_cells
        - mean_right * mean_right
        + variance_bias
    )
    covariance = box_sum(left_field * right_field, row_count) / box_cells - mean_left * mean_right
    denom_root = jnp.sqrt(var_left * var_right)
    ncc_value = covariance / denom_root
    g_cov = -weight / denom_root
    g_left = weight * ncc_value / (2.0 * var_left)
    g_right = weight * ncc_value / (2.0 * var_right)
    h_left = -g_cov * mean_right - 2.0 * g_left * mean_left
    h_right = -g_cov * mean_left - 2.0 * g_right * mean_right
    stacked = jnp.stack([g_cov, g_left, g_right, h_left, h_right])
    widened = padded_2(stacked.astype(jnp.bfloat16), (("strip", 1),), RADIUS).astype(stacked.dtype)
    boxed = box_sum(widened, row_count)
    mid_left = left_field[depth : depth + row_count]
    mid_right = right_field[depth : depth + row_count]
    grad_left = (boxed[3] + 2.0 * mid_left * boxed[1] + mid_right * boxed[0]) / box_cells
    grad_right = (boxed[4] + 2.0 * mid_right * boxed[2] + mid_left * boxed[0]) / box_cells
    return (grad_left, grad_right)


def per_device(images, row_weights, row_shift, col_weights, col_shift, pair_on):
    sec_count, row_count, col_count = images.shape
    sec_pos = lax.axis_index("sec")
    total_sections = sec_count * lax.axis_size("sec")
    source_depth = MAX_SHIFT + 2
    source = padded_2(images, (("strip", 1),), source_depth)

    def warp_rows(source_sec, weights, shift_value):
        running = jnp.zeros((row_count, col_count), jnp.float32)
        for tap_index in range(TAP_COUNT):
            window = lax.dynamic_slice_in_dim(
                source_sec, source_depth - 1 + tap_index + shift_value, row_count, 0
            )
            running = running + weights[tap_index][:, None] * window.astype(jnp.float32)
        return running.astype(jnp.bfloat16)

    row_warped = jax.vmap(warp_rows)(source, row_weights, row_shift[:, 0])
    row_ids = lax.broadcasted_iota(jnp.int32, (col_count, col_count), 0)
    col_ids = lax.broadcasted_iota(jnp.int32, (col_count, col_count), 1)

    def column_matrix(weights, shift_value):
        offsets = row_ids - col_ids - shift_value + 1
        matrix = jnp.zeros((col_count, col_count), jnp.bfloat16)
        for tap_index in range(TAP_COUNT):
            matrix = jnp.where(offsets == tap_index, weights[tap_index][None, :], matrix)
        return matrix

    matrices = jax.vmap(column_matrix)(col_weights, col_shift)
    warped = jnp.einsum(
        "srw,swv->srv", row_warped, matrices, preferred_element_type=jnp.float32
    ).astype(jnp.bfloat16)
    depth = RADIUS
    rimmed = padded_2(warped, (("strip", 1),), depth)
    hops = (PAIR_REACH + sec_count - 1) // sec_count
    first_global = sec_pos * sec_count
    padded_on = jnp.concatenate([jnp.zeros((PAIR_REACH, PAIR_REACH), jnp.int32), pair_on], 0)
    on_rows = lax.dynamic_slice_in_dim(padded_on, first_global, sec_count + PAIR_REACH, 0).astype(
        jnp.float32
    )
    pieces = {}
    section = 0
    pieces[section] = rimmed[section]
    for hop in range(1, hops + 1):
        arrived = passed_along(rimmed, "sec", -hop)
        slot_pos = 0
        pieces[hop * sec_count + slot_pos] = arrived[slot_pos]
    gradient_sums = {}
    section = 0
    for distance in range(1, PAIR_REACH + 1):
        global_first = first_global + section
        inside = (global_first >= 0) & (global_first + distance < total_sections)
        grad_left, grad_right = pair_grads(
            pieces[section],
            pieces[section + distance],
            on_rows[section + PAIR_REACH, distance - 1] * inside.astype(jnp.float32),
            depth,
            row_count,
        )
        for target, term in ((section, grad_left), (section + distance, grad_right)):
            if target in gradient_sums:
                gradient_sums[target] = gradient_sums[target] + term
            else:
                gradient_sums[target] = term
    section = 0
    own_grads = [gradient_sums[section]]
    for hop in range(1, hops + 1):
        parcel = jnp.stack([gradient_sums[hop * sec_count]])
        returned = passed_along(parcel, "sec", hop)
        slot_pos = 0
        own_grads[slot_pos] = own_grads[slot_pos] + returned[slot_pos]
    grad_warped = jnp.stack(own_grads)
    middle = rimmed[:, depth - 1 : depth + row_count + 1].astype(jnp.float32)
    slope_rows = (middle[:, 2:] - middle[:, :-2]) * 0.5
    centre = middle[:, 1:-1]
    side_padded = jnp.pad(centre, ((0, 0), (0, 0), (1, 1)))
    slope_cols = (side_padded[:, :, 2:] - side_padded[:, :, :-2]) * 0.5
    products = jnp.stack([grad_warped * slope_rows, grad_warped * slope_cols])
    widened = padded_2(products, (("strip", 2),), RADIUS)
    displacement = -box_sum(widened, row_count) / 9.0
    return (grad_warped, displacement)


MESH = pl.DeviceIdType.MESH
BLOCK = 16
LANES = 128
COL_TILE = 256


def rows_sum_from(x):
    m = x.shape[0]
    t = x + pltpu.roll(x, m - 1, 0) + pltpu.roll(x, m - 2, 0)
    t = t + pltpu.roll(t, m - 3, 0) + pltpu.roll(t, m - 6, 0)
    return t[: m - 2 * RADIUS]


def rows_sum_centred(x):
    m = x.shape[0]
    t = x + pltpu.roll(x, m - 1, 0) + pltpu.roll(x, 1, 0)
    return t + pltpu.roll(t, m - 3, 0) + pltpu.roll(t, 3, 0)


def with_zero_lanes(x):
    return jnp.concatenate([x, jnp.zeros((x.shape[0], LANES), x.dtype)], axis=1)


def cols_sum(x):
    width = x.shape[1]
    x = with_zero_lanes(x)
    m = width + LANES
    t = x + pltpu.roll(x, m - 1, 1) + pltpu.roll(x, 1, 1)
    t = t + pltpu.roll(t, m - 3, 1) + pltpu.roll(t, 3, 1)
    return t[:, :width]


def align_kernel(
    n,
    strips,
    images,
    row_weights,
    row_shift,
    col_weights,
    col_shift,
    pair_on,
    grad_out,
    disp_out,
    img_ext,
    col_mats,
    warp_ext,
    window,
    field,
    mean,
    inv,
    ncc_sum,
    mean_sum,
    grad_acc,
    grad_send,
    grad_ext,
    img_send,
    img_recv,
    halo_send,
    halo_recv,
    win_send,
    win_recv,
    back_send,
    back_recv,
    edge_send,
    edge_recv,
):
    me = lax.axis_index("sec")
    z = lax.axis_index("strip")
    rows, width = images.shape
    f32, bf16 = jnp.float32, jnp.bfloat16
    has_up = z > 0
    has_down = z < strips - 1
    up = {"strip": z - 1}
    down = {"strip": z + 1}
    cells = float((2 * RADIUS + 1) ** 2)

    def remote(src, dst, send, recv, where):
        return pltpu.make_async_remote_copy(
            src_ref=src, dst_ref=dst, send_sem=send, recv_sem=recv, device_id=where, device_id_type=MESH
        )

    barrier = pltpu.get_barrier_semaphore()
    for step in range(1, n):
        pl.semaphore_signal(
            barrier, inc=1, device_id={"sec": lax.rem(me + step, n)}, device_id_type=MESH
        )

    @pl.when(has_up)
    def _():
        pl.semaphore_signal(barrier, inc=1, device_id=up, device_id_type=MESH)

    @pl.when(has_down)
    def _():
        pl.semaphore_signal(barrier, inc=1, device_id=down, device_id_type=MESH)

    pl.semaphore_wait(barrier, n - 1 + jnp.where(has_up, 1, 0) + jnp.where(has_down, 1, 0))

    img_up = remote(
        images.at[pl.ds(0, BLOCK)], img_ext.at[pl.ds(rows + BLOCK, BLOCK)], img_send.at[0], img_recv.at[1], up
    )
    img_down = remote(
        images.at[pl.ds(rows - BLOCK, BLOCK)], img_ext.at[pl.ds(0, BLOCK)], img_send.at[1], img_recv.at[0], down
    )

    def exchange_start(to_up, to_down):
        @pl.when(has_up)
        def _():
            to_up.start()

        @pl.when(has_down)
        def _():
            to_down.start()

    def exchange_wait(to_up, to_down):
        @pl.when(has_up)
        def _():
            to_up.wait_send()
            to_down.wait_recv()

        @pl.when(has_down)
        def _():
            to_down.wait_send()
            to_up.wait_recv()

    exchange_start(img_up, img_down)
    zero_block = jnp.zeros((BLOCK, width), bf16)

    @pl.when(jnp.logical_not(has_up))
    def _():
        img_ext[0:BLOCK] = zero_block
        warp_ext[0] = zero_block
        grad_ext[0] = zero_block

    @pl.when(jnp.logical_not(has_down))
    def _():
        img_ext[rows + BLOCK : rows + 2 * BLOCK] = zero_block
        warp_ext[n + 1] = zero_block
        grad_ext[n + 1] = zero_block

    img_ext[BLOCK : rows + BLOCK] = images[...]
    col_move = col_shift[0]
    spans = []
    for tile in range(width // COL_TILE):
        first = max(0, tile * COL_TILE - LANES)
        last = min(width, (tile + 1) * COL_TILE + LANES)
        spans.append((first, last))
        extent = last - first
        row_ids = lax.broadcasted_iota(jnp.int32, (extent, COL_TILE), 0) + first
        col_ids = lax.broadcasted_iota(jnp.int32, (extent, COL_TILE), 1) + tile * COL_TILE
        offsets = row_ids - col_ids - col_move + 1
        matrix = jnp.zeros((extent, COL_TILE), f32)
        for tap in range(TAP_COUNT):
            taps = col_weights[tap : tap + 1, tile * COL_TILE : (tile + 1) * COL_TILE]
            matrix = jnp.where(offsets == tap, taps, matrix)
        col_mats[tile, 0:extent, :] = matrix.astype(bf16)

    ext = rows + 2 * BLOCK
    source_ids = lax.broadcasted_iota(jnp.int32, (ext, rows), 0)
    target_ids = lax.broadcasted_iota(jnp.int32, (ext, rows), 1)
    offsets = source_ids - target_ids - BLOCK - row_shift[0, 0] + 1
    row_matrix = jnp.zeros((ext, rows), f32)
    for tap in range(TAP_COUNT):
        row_matrix = jnp.where(offsets == tap, row_weights[tap : tap + 1, :], row_matrix)
    parts = []
    rest = row_matrix
    for _ in range(3):
        part = rest.astype(bf16)
        parts.append(part)
        rest = rest - part.astype(f32)

    exchange_wait(img_up, img_down)
    row_warped = jnp.zeros((rows, width), f32)
    for part in reversed(parts):
        row_warped = row_warped + lax.dot_general(
            part, img_ext[...], (((0,), (0,)), ((), ())), preferred_element_type=f32
        )
    row_warped = row_warped.astype(bf16)
    for tile, (first, last) in enumerate(spans):
        piece = jnp.dot(
            row_warped[:, first:last], col_mats[tile, 0 : last - first, :], preferred_element_type=f32
        ).astype(bf16)
        warp_ext[1 : n + 1, :, tile * COL_TILE : (tile + 1) * COL_TILE] = piece.reshape(n, BLOCK, COL_TILE)

    halo_up = remote(warp_ext.at[1], warp_ext.at[n + 1], halo_send.at[0], halo_recv.at[1], up)
    halo_down = remote(warp_ext.at[n], warp_ext.at[0], halo_send.at[1], halo_recv.at[0], down)
    exchange_start(halo_up, halo_down)

    def window_copy(target):
        return remote(
            warp_ext.at[pl.ds(target, 3)], window.at[me], win_send.at[target], win_recv.at[me], {"sec": target}
        )

    def window_start(target):
        @pl.when(target != me)
        def _():
            window_copy(target).start()

    for target in range(1, n - 1):
        window_start(target)
    exchange_wait(halo_up, halo_down)
    window_start(0)
    window_start(n - 1)
    window[me] = warp_ext[pl.ds(me, 3)]

    half = BLOCK // 2
    near = BLOCK + 2 * half
    mid_rows = BLOCK + 2 * RADIUS

    def statistics(step, carry):
        sec = lax.rem(me + step, n)

        @pl.when(sec != me)
        def _():
            remote(
                warp_ext.at[pl.ds(0, 3)], window.at[sec], win_send.at[sec], win_recv.at[sec], {"sec": sec}
            ).wait_recv()

        values = window[sec].reshape(3 * BLOCK, width).astype(f32)[half : half + near]
        field[sec] = values
        average = cols_sum(rows_sum_from(values)) * (1.0 / cells)
        square = cols_sum(rows_sum_from(values * values)) * (1.0 / cells)
        mean[sec] = average
        inv[sec] = lax.rsqrt(square - average * average + variance_bias)
        ncc_sum[sec] = jnp.zeros((mid_rows, width), f32)
        mean_sum[sec] = jnp.zeros((mid_rows, width), f32)
        grad_acc[sec] = jnp.zeros((BLOCK, width), f32)
        return carry

    lax.fori_loop(0, n, statistics, 0)

    row_ids = lax.broadcasted_iota(jnp.int32, (mid_rows, width), 0) + (z * rows + me * BLOCK - RADIUS)
    inside = jnp.where((row_ids >= 0) & (row_ids < strips * rows), 1.0, 0.0).astype(f32)

    for distance in range(1, PAIR_REACH + 1):

        def one_pair(left, carry):
            right = left + distance
            weight = pair_on[left, distance - 1].astype(f32)
            a, b = field[left], field[right]
            mean_a, mean_b = mean[left], mean[right]
            cov = cols_sum(rows_sum_from(a * b)) * (1.0 / cells) - mean_a * mean_b
            scale = inv[left] * inv[right] * (inside * weight)
            ncc = cov * scale
            ncc_sum[left] += ncc
            ncc_sum[right] += ncc
            mean_sum[left] += scale * mean_b
            mean_sum[right] += scale * mean_a
            boxed = cols_sum(rows_sum_from(scale))
            grad_acc[left] += boxed * b[half : half + BLOCK]
            grad_acc[right] += boxed * a[half : half + BLOCK]
            return carry

        lax.fori_loop(0, n - distance, one_pair, 0)

    def back_copy(sec):
        return remote(
            grad_send.at[sec], grad_ext.at[me + 1], back_send.at[sec], back_recv.at[me], {"sec": sec}
        )

    def finish(step, carry):
        sec = lax.rem(me + 1 + step, n)
        root = inv[sec]
        g_twice = ncc_sum[sec] * root * root
        h = mean_sum[sec] - mean[sec] * g_twice
        boxed_h = cols_sum(rows_sum_from(h))
        boxed_g = cols_sum(rows_sum_from(g_twice))
        mid = field[sec, half : half + BLOCK, :]
        total = (boxed_h + mid * boxed_g - grad_acc[sec]) * (1.0 / cells)
        grad_send[sec] = total.astype(bf16)

        @pl.when(sec != me)
        def _():
            back_copy(sec).start()

        return carry

    lax.fori_loop(0, n, finish, 0)
    grad_ext[me + 1] = grad_send[me]

    def back_wait(step, carry):
        sec = lax.rem(me + step, n)
        remote(
            grad_send.at[sec], grad_ext.at[sec + 1], back_send.at[sec], back_recv.at[sec], {"sec": sec}
        ).wait_recv()
        return carry

    lax.fori_loop(1, n, back_wait, 0)
    edge_up = remote(grad_ext.at[1], grad_ext.at[n + 1], edge_send.at[0], edge_recv.at[1], up)
    edge_down = remote(grad_ext.at[n], grad_ext.at[0], edge_send.at[1], edge_recv.at[0], down)
    exchange_start(edge_up, edge_down)

    def displace(block):
        grads = grad_ext[pl.ds(block, 3)].reshape(3 * BLOCK, width).astype(f32)
        warped = warp_ext[pl.ds(block, 3)].reshape(3 * BLOCK, width).astype(f32)
        out_rows = pl.ds(pl.multiple_of(block * BLOCK, BLOCK), BLOCK)
        grad_out[0, out_rows, :] = grads[BLOCK : 2 * BLOCK]
        span = 3 * BLOCK
        slope_rows = (pltpu.roll(warped, span - 1, 0) - pltpu.roll(warped, 1, 0))[half : half + near]
        padded = with_zero_lanes(warped[half : half + near])
        lanes = width + LANES
        slope_cols = (pltpu.roll(padded, lanes - 1, 1) - pltpu.roll(padded, 1, 1))[:, :width]
        near_grads = grads[half : half + near] * (-0.5 / 9.0)
        for part, slope in enumerate((slope_rows, slope_cols)):
            summed = rows_sum_centred(near_grads * slope)[half : half + BLOCK]
            disp_out[part, 0, out_rows, :] = cols_sum(summed)

    def displace_step(block, carry):
        displace(block)
        return carry

    lax.fori_loop(1, n - 1, displace_step, 0)
    exchange_wait(edge_up, edge_down)

    def displace_end(step, carry):
        displace(step * (n - 1))
        return carry

    lax.fori_loop(0, 2, displace_end, 0)

    def drain(step, carry):
        sec = lax.rem(me + step, n)
        window_copy(sec).wait_send()
        back_copy(sec).wait_send()
        return carry

    lax.fori_loop(1, n, drain, 0)


def fused(n, strips, images, row_weights, row_shift, col_weights, col_shift, pair_on):
    _, rows, width = images.shape
    f32, bf16 = jnp.float32, jnp.bfloat16
    mid_rows = BLOCK + 2 * RADIUS
    vmem = pl.BlockSpec(memory_space=pltpu.VMEM)
    smem = pl.BlockSpec(memory_space=pltpu.SMEM)
    dma = pltpu.SemaphoreType.DMA
    return pl.pallas_call(
        functools.partial(align_kernel, n, strips),
        out_shape=(
            jax.ShapeDtypeStruct((1, rows, width), f32),
            jax.ShapeDtypeStruct((2, 1, rows, width), f32),
        ),
        in_specs=[vmem, vmem, smem, vmem, smem, smem],
        out_specs=(vmem, vmem),
        scratch_shapes=[
            pltpu.VMEM((rows + 2 * BLOCK, width), bf16),
            pltpu.VMEM((width // COL_TILE, COL_TILE + 2 * LANES, COL_TILE), bf16),
            pltpu.VMEM((n + 2, BLOCK, width), bf16),
            pltpu.VMEM((n, 3, BLOCK, width), bf16),
            pltpu.VMEM((n, 2 * BLOCK, width), f32),
            pltpu.VMEM((n, mid_rows, width), f32),
            pltpu.VMEM((n, mid_rows, width), f32),
            pltpu.VMEM((n, mid_rows, width), f32),
            pltpu.VMEM((n, mid_rows, width), f32),
            pltpu.VMEM((n, BLOCK, width), f32),
            pltpu.VMEM((n, BLOCK, width), bf16),
            pltpu.VMEM((n + 2, BLOCK, width), bf16),
            dma((2,)),
            dma((2,)),
            dma((2,)),
            dma((2,)),
            dma((n,)),
            dma((n,)),
            dma((n,)),
            dma((n,)),
            dma((2,)),
            dma((2,)),
        ],
        compiler_params=pltpu.CompilerParams(
            collective_id=0, has_side_effects=True, vmem_limit_bytes=40 * 1024 * 1024
        ),
    )(images[0], row_weights[0], row_shift, col_weights[0].astype(f32), col_shift, pair_on)


def solution(mesh):
    n, strips = mesh.shape["sec"], mesh.shape["strip"]

    def step(images, *rest):
        sections, rows, width = images.shape
        if sections == 1 and rows == n * BLOCK and width % COL_TILE == 0:
            return fused(n, strips, images, *rest)
        return per_device(images, *rest)

    return jax.shard_map(
        step,
        mesh=mesh,
        in_specs=(
            P("sec", "strip", None),
            P("sec", None, "strip"),
            P("sec", "strip"),
            P("sec", None, None),
            P("sec"),
            P(),
        ),
        out_specs=(P("sec", "strip", None), P(None, "sec", "strip", None)),
        check_vma=False,
    )
```

```python
import functools

import jax
import jax.numpy as jnp
from jax import lax
from jax.experimental import pallas as pl
from jax.experimental.pallas import tpu as pltpu
from jax.sharding import PartitionSpec as P

TAP_COUNT = 4
MAX_SHIFT = 4
RADIUS = 4
PAIR_REACH = 3


variance_bias = 0.25


def padded_2(block, sides, width):
    for axis, dim in sides:
        count = lax.axis_size(axis)
        forward = [(i, i + 1) for i in range(count - 1)]
        backward = [(target, source) for source, target in forward]
        low = lax.ppermute(
            lax.slice_in_dim(block, block.shape[dim] - width, None, axis=dim), axis, forward
        )
        high = lax.ppermute(lax.slice_in_dim(block, 0, width, axis=dim), axis, backward)
        block = jnp.concatenate([low, block, high], axis=dim)
    return block


def passed_along(value, axis, steps):
    count = lax.axis_size(axis)
    initial, last = (max(0, -steps), min(count, count - steps))
    return lax.ppermute(value, axis, [(source, source + steps) for source in range(initial, last)])


def box_rows(field, out_rows):
    running = field[..., 0:out_rows, :]
    for step_row in range(1, 2 * RADIUS + 1):
        running = running + field[..., step_row : step_row + out_rows, :]
    return running


def box_cols(field):
    col_count = field.shape[-1]
    widths = [(0, 0)] * (field.ndim - 1) + [(RADIUS, RADIUS)]
    padded = jnp.pad(field, widths)
    running = padded[..., 0:col_count]
    for step_col in range(1, 2 * RADIUS + 1):
        running = running + padded[..., step_col : step_col + col_count]
    return running


def box_sum(field, out_rows):
    return box_cols(box_rows(field, out_rows))


def pair_grads(left_rim, right_rim, weight, depth, row_count):
    box_cells = float((2 * RADIUS + 1) ** 2)
    left_field = left_rim.astype(jnp.float32)
    right_field = right_rim.astype(jnp.float32)
    mean_left = box_sum(left_field, row_count) / box_cells
    mean_right = box_sum(right_field, row_count) / box_cells
    var_left = (
        box_sum(left_field * left_field, row_count) / box_cells
        - mean_left * mean_left
        + variance_bias
    )
    var_right = (
        box_sum(right_field * right_field, row_count) / box_cells
        - mean_right * mean_right
        + variance_bias
    )
    covariance = box_sum(left_field * right_field, row_count) / box_cells - mean_left * mean_right
    denom_root = jnp.sqrt(var_left * var_right)
    ncc_value = covariance / denom_root
    g_cov = -weight / denom_root
    g_left = weight * ncc_value / (2.0 * var_left)
    g_right = weight * ncc_value / (2.0 * var_right)
    h_left = -g_cov * mean_right - 2.0 * g_left * mean_left
    h_right = -g_cov * mean_left - 2.0 * g_right * mean_right
    stacked = jnp.stack([g_cov, g_left, g_right, h_left, h_right])
    widened = padded_2(stacked.astype(jnp.bfloat16), (("strip", 1),), RADIUS).astype(stacked.dtype)
    boxed = box_sum(widened, row_count)
    mid_left = left_field[depth : depth + row_count]
    mid_right = right_field[depth : depth + row_count]
    grad_left = (boxed[3] + 2.0 * mid_left * boxed[1] + mid_right * boxed[0]) / box_cells
    grad_right = (boxed[4] + 2.0 * mid_right * boxed[2] + mid_left * boxed[0]) / box_cells
    return (grad_left, grad_right)


def per_device(images, row_weights, row_shift, col_weights, col_shift, pair_on):
    sec_count, row_count, col_count = images.shape
    sec_pos = lax.axis_index("sec")
    total_sections = sec_count * lax.axis_size("sec")
    source_depth = MAX_SHIFT + 2
    source = padded_2(images, (("strip", 1),), source_depth)

    def warp_rows(source_sec, weights, shift_value):
        running = jnp.zeros((row_count, col_count), jnp.float32)
        for tap_index in range(TAP_COUNT):
            window = lax.dynamic_slice_in_dim(
                source_sec, source_depth - 1 + tap_index + shift_value, row_count, 0
            )
            running = running + weights[tap_index][:, None] * window.astype(jnp.float32)
        return running.astype(jnp.bfloat16)

    row_warped = jax.vmap(warp_rows)(source, row_weights, row_shift[:, 0])
    row_ids = lax.broadcasted_iota(jnp.int32, (col_count, col_count), 0)
    col_ids = lax.broadcasted_iota(jnp.int32, (col_count, col_count), 1)

    def column_matrix(weights, shift_value):
        offsets = row_ids - col_ids - shift_value + 1
        matrix = jnp.zeros((col_count, col_count), jnp.bfloat16)
        for tap_index in range(TAP_COUNT):
            matrix = jnp.where(offsets == tap_index, weights[tap_index][None, :], matrix)
        return matrix

    matrices = jax.vmap(column_matrix)(col_weights, col_shift)
    warped = jnp.einsum(
        "srw,swv->srv", row_warped, matrices, preferred_element_type=jnp.float32
    ).astype(jnp.bfloat16)
    depth = RADIUS
    rimmed = padded_2(warped, (("strip", 1),), depth)
    hops = (PAIR_REACH + sec_count - 1) // sec_count
    first_global = sec_pos * sec_count
    padded_on = jnp.concatenate([jnp.zeros((PAIR_REACH, PAIR_REACH), jnp.int32), pair_on], 0)
    on_rows = lax.dynamic_slice_in_dim(padded_on, first_global, sec_count + PAIR_REACH, 0).astype(
        jnp.float32
    )
    pieces = {}
    section = 0
    pieces[section] = rimmed[section]
    for hop in range(1, hops + 1):
        arrived = passed_along(rimmed, "sec", -hop)
        slot_pos = 0
        pieces[hop * sec_count + slot_pos] = arrived[slot_pos]
    gradient_sums = {}
    section = 0
    for distance in range(1, PAIR_REACH + 1):
        global_first = first_global + section
        inside = (global_first >= 0) & (global_first + distance < total_sections)
        grad_left, grad_right = pair_grads(
            pieces[section],
            pieces[section + distance],
            on_rows[section + PAIR_REACH, distance - 1] * inside.astype(jnp.float32),
            depth,
            row_count,
        )
        for target, term in ((section, grad_left), (section + distance, grad_right)):
            if target in gradient_sums:
                gradient_sums[target] = gradient_sums[target] + term
            else:
                gradient_sums[target] = term
    section = 0
    own_grads = [gradient_sums[section]]
    for hop in range(1, hops + 1):
        parcel = jnp.stack([gradient_sums[hop * sec_count]])
        returned = passed_along(parcel, "sec", hop)
        slot_pos = 0
        own_grads[slot_pos] = own_grads[slot_pos] + returned[slot_pos]
    grad_warped = jnp.stack(own_grads)
    middle = rimmed[:, depth - 1 : depth + row_count + 1].astype(jnp.float32)
    slope_rows = (middle[:, 2:] - middle[:, :-2]) * 0.5
    centre = middle[:, 1:-1]
    side_padded = jnp.pad(centre, ((0, 0), (0, 0), (1, 1)))
    slope_cols = (side_padded[:, :, 2:] - side_padded[:, :, :-2]) * 0.5
    products = jnp.stack([grad_warped * slope_rows, grad_warped * slope_cols])
    widened = padded_2(products, (("strip", 2),), RADIUS)
    displacement = -box_sum(widened, row_count) / 9.0
    return (grad_warped, displacement)


MESH = pl.DeviceIdType.MESH
BLOCK = 16
HALF_ROWS = BLOCK // 2
LANES = 128
COL_TILE = 256


def rows_sum_from(x):
    m = x.shape[0]
    t = x + pltpu.roll(x, m - 1, 0) + pltpu.roll(x, m - 2, 0)
    t = t + pltpu.roll(t, m - 3, 0) + pltpu.roll(t, m - 6, 0)
    return t[: m - 2 * RADIUS]


def rows_sum_centred(x):
    m = x.shape[0]
    t = x + pltpu.roll(x, m - 1, 0) + pltpu.roll(x, 1, 0)
    return t + pltpu.roll(t, m - 3, 0) + pltpu.roll(t, 3, 0)


def with_zero_lanes(x):
    return jnp.concatenate([x, jnp.zeros((x.shape[0], LANES), x.dtype)], axis=1)


def cols_sum(x):
    width = x.shape[1]
    x = with_zero_lanes(x)
    m = width + LANES
    t = x + pltpu.roll(x, m - 1, 1) + pltpu.roll(x, 1, 1)
    t = t + pltpu.roll(t, m - 3, 1) + pltpu.roll(t, 3, 1)
    return t[:, :width]


def halves_to_rows(x):
    x = x.astype(jnp.float32)
    count, _, half = x.shape
    rows = jnp.concatenate([x[:, :HALF_ROWS], x[:, HALF_ROWS:]], axis=2)
    return rows.reshape(count * HALF_ROWS, 2 * half)


def align_kernel(
    n,
    strips,
    images,
    row_weights,
    row_shift,
    col_weights,
    col_shift,
    pair_on,
    grad_done,
    warp_done,
    grad_ext,
    warp_ext,
    img_ext,
    col_mats,
    window,
    field,
    mean,
    inv,
    ncc_sum,
    mean_sum,
    grad_acc,
    grad_send,
    img_send,
    img_recv,
    halo_send,
    halo_recv,
    win_send,
    win_recv,
    back_send,
    back_recv,
    edge_send,
    edge_recv,
):
    me = lax.axis_index("sec")
    z = lax.axis_index("strip")
    rows, width = images.shape
    f32, bf16 = jnp.float32, jnp.bfloat16
    has_up = z > 0
    has_down = z < strips - 1
    up = {"strip": z - 1}
    down = {"strip": z + 1}
    cells = float((2 * RADIUS + 1) ** 2)


    def remote(src, dst, send, recv, where):
        return pltpu.make_async_remote_copy(
            src_ref=src, dst_ref=dst, send_sem=send, recv_sem=recv, device_id=where, device_id_type=MESH
        )

    barrier = pltpu.get_barrier_semaphore()
    for step in range(1, n):
        pl.semaphore_signal(
            barrier, inc=1, device_id={"sec": lax.rem(me + step, n)}, device_id_type=MESH
        )

    @pl.when(has_up)
    def _():
        pl.semaphore_signal(barrier, inc=1, device_id=up, device_id_type=MESH)

    @pl.when(has_down)
    def _():
        pl.semaphore_signal(barrier, inc=1, device_id=down, device_id_type=MESH)

    pl.semaphore_wait(barrier, n - 1 + jnp.where(has_up, 1, 0) + jnp.where(has_down, 1, 0))

    img_up = remote(
        images.at[pl.ds(0, BLOCK)], img_ext.at[pl.ds(rows + BLOCK, BLOCK)], img_send.at[0], img_recv.at[1], up
    )
    img_down = remote(
        images.at[pl.ds(rows - BLOCK, BLOCK)], img_ext.at[pl.ds(0, BLOCK)], img_send.at[1], img_recv.at[0], down
    )

    def exchange_start(to_up, to_down):
        @pl.when(has_up)
        def _():
            to_up.start()

        @pl.when(has_down)
        def _():
            to_down.start()

    def exchange_wait(to_up, to_down):
        @pl.when(has_up)
        def _():
            to_up.wait_send()
            to_down.wait_recv()

        @pl.when(has_down)
        def _():
            to_down.wait_send()
            to_up.wait_recv()

    exchange_start(img_up, img_down)
    zero_block = jnp.zeros((BLOCK, width), bf16)
    zero_half = jnp.zeros((BLOCK, width // 2), bf16)
    bottom = 2 * n + 1

    @pl.when(jnp.logical_not(has_up))
    def _():
        img_ext[0:BLOCK] = zero_block
        warp_ext[0] = zero_half
        grad_ext[0] = zero_block

    @pl.when(jnp.logical_not(has_down))
    def _():
        img_ext[rows + BLOCK : rows + 2 * BLOCK] = zero_block
        warp_ext[bottom] = zero_half
        grad_ext[n + 1] = zero_block

    col_move = col_shift[0]
    all_taps = col_weights[...].astype(f32)
    spans = []
    tiles = width // COL_TILE
    for tile in range(tiles):
        first = max(0, tile * COL_TILE - LANES)
        last = min(width, (tile + 1) * COL_TILE + LANES)
        spans.append((first, last))
        extent = last - first
        row_ids = lax.broadcasted_iota(jnp.int32, (extent, COL_TILE), 0) + first
        col_ids = lax.broadcasted_iota(jnp.int32, (extent, COL_TILE), 1) + tile * COL_TILE
        offsets = row_ids - col_ids - col_move + 1
        matrix = jnp.zeros((extent, COL_TILE), f32)
        for tap in range(TAP_COUNT):
            taps = all_taps[tap : tap + 1, tile * COL_TILE : (tile + 1) * COL_TILE]
            matrix = jnp.where(offsets == tap, taps, matrix)
        col_mats[tile, 0:extent, :] = matrix.astype(bf16)

    ext = rows + 2 * BLOCK
    source_ids = lax.broadcasted_iota(jnp.int32, (ext, rows), 0)
    target_ids = lax.broadcasted_iota(jnp.int32, (ext, rows), 1)
    offsets = source_ids - target_ids - BLOCK - row_shift[0, 0] + 1
    row_matrix = jnp.zeros((ext, rows), f32)
    for tap in range(TAP_COUNT):
        row_matrix = jnp.where(offsets == tap, row_weights[tap : tap + 1, :], row_matrix)
    parts = []
    rest = row_matrix
    for _ in range(3):
        part = rest.astype(bf16)
        parts.append(part)
        rest = rest - part.astype(f32)

    img_ext[BLOCK : rows + BLOCK] = images[...]
    exchange_wait(img_up, img_down)
    row_warped = jnp.zeros((rows, width), f32)
    for part in reversed(parts):
        row_warped = row_warped + lax.dot_general(
            part, img_ext[...], (((0,), (0,)), ((), ())), preferred_element_type=f32
        )
    row_warped = row_warped.astype(bf16)

    def warped_tile(tile):
        first, last = spans[tile]
        piece = jnp.dot(
            row_warped[:, first:last], col_mats[tile, 0 : last - first, :], preferred_element_type=f32
        )
        return piece.reshape(2 * n, HALF_ROWS, COL_TILE)

    for tile in range(tiles // 2):
        both = jnp.concatenate([warped_tile(tile), warped_tile(tile + tiles // 2)], axis=1)
        warp_ext[1:bottom, :, tile * COL_TILE : (tile + 1) * COL_TILE] = both.astype(bf16)

    halo_up = remote(warp_ext.at[1], warp_ext.at[bottom], halo_send.at[0], halo_recv.at[1], up)
    halo_down = remote(warp_ext.at[bottom - 1], warp_ext.at[0], halo_send.at[1], halo_recv.at[0], down)
    exchange_start(halo_up, halo_down)

    def window_copy(target):
        return remote(
            warp_ext.at[pl.ds(2 * target, 4)], window.at[me], win_send.at[target], win_recv.at[me], {"sec": target}
        )

    def send_inner(step, carry):
        target = lax.rem(me + n - step, n)

        @pl.when((target > 0) & (target < n - 1))
        def _():
            window_copy(target).start()

        return carry

    def send_outer(step, carry):
        target = lax.rem(me + n - step, n)

        @pl.when((target == 0) | (target == n - 1))
        def _():
            window_copy(target).start()

        return carry

    lax.fori_loop(1, n, send_inner, 0)
    exchange_wait(halo_up, halo_down)
    lax.fori_loop(1, n, send_outer, 0)
    window[me] = warp_ext[pl.ds(2 * me, 4)]

    mid_rows = BLOCK + 2 * RADIUS
    row_ids = lax.broadcasted_iota(jnp.int32, (mid_rows, width), 0) + (z * rows + me * BLOCK - RADIUS)
    inside = jnp.where((row_ids >= 0) & (row_ids < strips * rows), 1.0, 0.0).astype(f32)

    def one_pair(left, right, distance):
        weight = pair_on[left, distance - 1].astype(f32)
        a, b = field[left], field[right]
        mean_a, mean_b = mean[left], mean[right]
        cov = cols_sum(rows_sum_from(a * b)) * (1.0 / cells) - mean_a * mean_b
        scale = inv[left] * inv[right] * (inside * weight)
        ncc = cov * scale
        ncc_sum[left] += ncc
        ncc_sum[right] += ncc
        mean_sum[left] += scale * mean_b
        mean_sum[right] += scale * mean_a
        boxed = cols_sum(rows_sum_from(scale))
        grad_acc[left] += boxed * b[HALF_ROWS : HALF_ROWS + BLOCK]
        grad_acc[right] += boxed * a[HALF_ROWS : HALF_ROWS + BLOCK]

    def meet(step, carry):
        sec = lax.rem(me + step, n)

        @pl.when(step > 0)
        def _():
            remote(
                warp_ext.at[pl.ds(0, 4)], window.at[sec], win_send.at[sec], win_recv.at[sec], {"sec": sec}
            ).wait_recv()

        values = halves_to_rows(window[sec])
        field[sec] = values
        average = cols_sum(rows_sum_from(values)) * (1.0 / cells)
        square = cols_sum(rows_sum_from(values * values)) * (1.0 / cells)
        mean[sec] = average
        inv[sec] = lax.rsqrt(square - average * average + variance_bias)
        ncc_sum[sec] = jnp.zeros((mid_rows, width), f32)
        mean_sum[sec] = jnp.zeros((mid_rows, width), f32)
        grad_acc[sec] = jnp.zeros((BLOCK, width), f32)

        def with_earlier(distance, carry):
            @pl.when((sec >= distance) & (lax.rem(sec - distance - me + 2 * n, n) < step))
            def _():
                one_pair(lax.rem(sec - distance + n, n), sec, distance)

            @pl.when((sec + distance < n) & (lax.rem(sec + distance - me + 2 * n, n) < step))
            def _():
                one_pair(sec, lax.rem(sec + distance, n), distance)

            return carry

        lax.fori_loop(1, PAIR_REACH + 1, with_earlier, 0)
        return carry

    lax.fori_loop(0, n, meet, 0)

    def back_copy(sec):
        return remote(
            grad_send.at[sec], grad_ext.at[me + 1], back_send.at[sec], back_recv.at[me], {"sec": sec}
        )

    def finish(step, carry):
        sec = lax.rem(me + 1 + step, n)
        root = inv[sec]
        g_twice = ncc_sum[sec] * root * root
        h = mean_sum[sec] - mean[sec] * g_twice
        boxed_h = cols_sum(rows_sum_from(h))
        boxed_g = cols_sum(rows_sum_from(g_twice))
        mid = field[sec, HALF_ROWS : HALF_ROWS + BLOCK, :]
        total = (boxed_h + mid * boxed_g - grad_acc[sec]) * (1.0 / cells)
        grad_send[sec] = total.astype(bf16)

        @pl.when(sec != me)
        def _():
            back_copy(sec).start()

        return carry

    lax.fori_loop(0, n, finish, 0)
    grad_ext[me + 1] = grad_send[me]

    def drain(step, carry):
        sec = lax.rem(me + step, n)

        @pl.when(step > 0)
        def _():
            window_copy(sec).wait_send()
            back_copy(sec).wait_send()
            remote(
                grad_send.at[sec], grad_ext.at[sec + 1], back_send.at[sec], back_recv.at[sec], {"sec": sec}
            ).wait_recv()

        return carry

    lax.fori_loop(0, n, drain, 0)

    edge_up = remote(grad_ext.at[1], grad_ext.at[n + 1], edge_send.at[0], edge_recv.at[1], up)
    edge_down = remote(grad_ext.at[n], grad_ext.at[0], edge_send.at[1], edge_recv.at[0], down)
    exchange_start(edge_up, edge_down)
    exchange_wait(edge_up, edge_down)
    grad_done[...] = grad_ext[...]
    warp_done[...] = warp_ext[...]


def displace_kernel(n, grad_ext, warp_ext, grad_out, disp_out, grad_rows, disp_rows, grad_sems, disp_sems):
    _, rows, width = grad_rows.shape
    f32 = jnp.float32

    def copies(block):
        out_rows = pl.ds(pl.multiple_of(block * BLOCK, BLOCK), BLOCK)
        return [
            pltpu.make_async_copy(grad_rows.at[:, out_rows], grad_out.at[:, out_rows], grad_sems.at[block]),
            pltpu.make_async_copy(disp_rows.at[:, :, out_rows], disp_out.at[:, :, out_rows], disp_sems.at[block]),
        ]

    def displace(block, carry):
        near = BLOCK + 2 * HALF_ROWS
        grads = grad_ext[pl.ds(block, 3)].reshape(3 * BLOCK, width).astype(f32)
        warped = halves_to_rows(warp_ext[pl.ds(2 * block, 4)])
        out_rows = pl.ds(pl.multiple_of(block * BLOCK, BLOCK), BLOCK)
        grad_rows[0, out_rows, :] = grads[BLOCK : 2 * BLOCK]
        slope_rows = pltpu.roll(warped, near - 1, 0) - pltpu.roll(warped, 1, 0)
        padded = with_zero_lanes(warped)
        lanes = width + LANES
        slope_cols = (pltpu.roll(padded, lanes - 1, 1) - pltpu.roll(padded, 1, 1))[:, :width]
        near_grads = grads[HALF_ROWS : HALF_ROWS + near] * (-0.5 / 9.0)
        for part, slope in enumerate((slope_rows, slope_cols)):
            summed = rows_sum_centred(near_grads * slope)[HALF_ROWS : HALF_ROWS + BLOCK]
            disp_rows[part, 0, out_rows, :] = cols_sum(summed)
        for copy in copies(block):
            copy.start()
        return carry

    lax.fori_loop(0, n, displace, 0)

    def drain(block, carry):
        for copy in copies(block):
            copy.wait()
        return carry

    lax.fori_loop(0, n, drain, 0)


def fused(n, strips, images, row_weights, row_shift, col_weights, col_shift, pair_on):
    _, rows, width = images.shape
    f32, bf16 = jnp.float32, jnp.bfloat16
    mid_rows = BLOCK + 2 * RADIUS
    vmem = pl.BlockSpec(memory_space=pltpu.VMEM)
    smem = pl.BlockSpec(memory_space=pltpu.SMEM)
    where = pl.BlockSpec(memory_space=pltpu.HBM)
    dma = pltpu.SemaphoreType.DMA
    grad_ext, warp_ext = pl.pallas_call(
        functools.partial(align_kernel, n, strips),
        out_shape=(
            jax.ShapeDtypeStruct((n + 2, BLOCK, width), bf16),
            jax.ShapeDtypeStruct((2 * n + 2, BLOCK, width // 2), bf16),
        ),
        in_specs=[vmem, vmem, smem, vmem, smem, smem],
        out_specs=(vmem, vmem),
        scratch_shapes=[
            pltpu.VMEM((n + 2, BLOCK, width), bf16),
            pltpu.VMEM((2 * n + 2, BLOCK, width // 2), bf16),
            pltpu.VMEM((rows + 2 * BLOCK, width), bf16),
            pltpu.VMEM((width // COL_TILE, COL_TILE + 2 * LANES, COL_TILE), bf16),
            pltpu.VMEM((n, 4, BLOCK, width // 2), bf16),
            pltpu.VMEM((n, 2 * BLOCK, width), f32),
            pltpu.VMEM((n, mid_rows, width), f32),
            pltpu.VMEM((n, mid_rows, width), f32),
            pltpu.VMEM((n, mid_rows, width), f32),
            pltpu.VMEM((n, mid_rows, width), f32),
            pltpu.VMEM((n, BLOCK, width), f32),
            pltpu.VMEM((n, BLOCK, width), bf16),
            dma((2,)),
            dma((2,)),
            dma((2,)),
            dma((2,)),
            dma((n,)),
            dma((n,)),
            dma((n,)),
            dma((n,)),
            dma((n,)),
            dma((2,)),
        ],
        compiler_params=pltpu.CompilerParams(
            collective_id=0, has_side_effects=True, vmem_limit_bytes=40 * 1024 * 1024
        ),
    )(images[0], row_weights[0], row_shift, col_weights[0], col_shift, pair_on)
    return pl.pallas_call(
        functools.partial(displace_kernel, n),
        out_shape=(
            jax.ShapeDtypeStruct((1, rows, width), f32),
            jax.ShapeDtypeStruct((2, 1, rows, width), f32),
        ),
        in_specs=[vmem, vmem],
        out_specs=(where, where),
        scratch_shapes=[
            pltpu.VMEM((1, rows, width), f32),
            pltpu.VMEM((2, 1, rows, width), f32),
            dma((n,)),
            dma((n,)),
        ],
        compiler_params=pltpu.CompilerParams(vmem_limit_bytes=40 * 1024 * 1024),
    )(grad_ext, warp_ext)


def solution(mesh):
    n, strips = mesh.shape["sec"], mesh.shape["strip"]

    def step(images, *rest):
        sections, rows, width = images.shape
        if sections == 1 and rows == n * BLOCK and width % (2 * COL_TILE) == 0:
            return fused(n, strips, images, *rest)
        return per_device(images, *rest)

    return jax.shard_map(
        step,
        mesh=mesh,
        in_specs=(
            P("sec", "strip", None),
            P("sec", None, "strip"),
            P("sec", "strip"),
            P("sec", None, None),
            P("sec"),
            P(),
        ),
        out_specs=(P("sec", "strip", None), P(None, "sec", "strip", None)),
        check_vma=False,
    )
```

```python
import functools

import jax
import jax.numpy as jnp
from jax import lax
from jax.experimental import pallas as pl
from jax.experimental.pallas import tpu as pltpu
from jax.sharding import PartitionSpec as P

TAP_COUNT = 4
MAX_SHIFT = 4
RADIUS = 4
PAIR_REACH = 3


variance_bias = 0.25


def padded_2(block, sides, width):
    for axis, dim in sides:
        count = lax.axis_size(axis)
        forward = [(i, i + 1) for i in range(count - 1)]
        backward = [(target, source) for source, target in forward]
        low = lax.ppermute(
            lax.slice_in_dim(block, block.shape[dim] - width, None, axis=dim), axis, forward
        )
        high = lax.ppermute(lax.slice_in_dim(block, 0, width, axis=dim), axis, backward)
        block = jnp.concatenate([low, block, high], axis=dim)
    return block


def passed_along(value, axis, steps):
    count = lax.axis_size(axis)
    initial, last = (max(0, -steps), min(count, count - steps))
    return lax.ppermute(value, axis, [(source, source + steps) for source in range(initial, last)])


def box_rows(field, out_rows):
    running = field[..., 0:out_rows, :]
    for step_row in range(1, 2 * RADIUS + 1):
        running = running + field[..., step_row : step_row + out_rows, :]
    return running


def box_cols(field):
    col_count = field.shape[-1]
    widths = [(0, 0)] * (field.ndim - 1) + [(RADIUS, RADIUS)]
    padded = jnp.pad(field, widths)
    running = padded[..., 0:col_count]
    for step_col in range(1, 2 * RADIUS + 1):
        running = running + padded[..., step_col : step_col + col_count]
    return running


def box_sum(field, out_rows):
    return box_cols(box_rows(field, out_rows))


def pair_grads(left_rim, right_rim, weight, depth, row_count):
    box_cells = float((2 * RADIUS + 1) ** 2)
    left_field = left_rim.astype(jnp.float32)
    right_field = right_rim.astype(jnp.float32)
    mean_left = box_sum(left_field, row_count) / box_cells
    mean_right = box_sum(right_field, row_count) / box_cells
    var_left = (
        box_sum(left_field * left_field, row_count) / box_cells
        - mean_left * mean_left
        + variance_bias
    )
    var_right = (
        box_sum(right_field * right_field, row_count) / box_cells
        - mean_right * mean_right
        + variance_bias
    )
    covariance = box_sum(left_field * right_field, row_count) / box_cells - mean_left * mean_right
    denom_root = jnp.sqrt(var_left * var_right)
    ncc_value = covariance / denom_root
    g_cov = -weight / denom_root
    g_left = weight * ncc_value / (2.0 * var_left)
    g_right = weight * ncc_value / (2.0 * var_right)
    h_left = -g_cov * mean_right - 2.0 * g_left * mean_left
    h_right = -g_cov * mean_left - 2.0 * g_right * mean_right
    stacked = jnp.stack([g_cov, g_left, g_right, h_left, h_right])
    widened = padded_2(stacked.astype(jnp.bfloat16), (("strip", 1),), RADIUS).astype(stacked.dtype)
    boxed = box_sum(widened, row_count)
    mid_left = left_field[depth : depth + row_count]
    mid_right = right_field[depth : depth + row_count]
    grad_left = (boxed[3] + 2.0 * mid_left * boxed[1] + mid_right * boxed[0]) / box_cells
    grad_right = (boxed[4] + 2.0 * mid_right * boxed[2] + mid_left * boxed[0]) / box_cells
    return (grad_left, grad_right)


def per_device(images, row_weights, row_shift, col_weights, col_shift, pair_on):
    sec_count, row_count, col_count = images.shape
    sec_pos = lax.axis_index("sec")
    total_sections = sec_count * lax.axis_size("sec")
    source_depth = MAX_SHIFT + 2
    source = padded_2(images, (("strip", 1),), source_depth)

    def warp_rows(source_sec, weights, shift_value):
        running = jnp.zeros((row_count, col_count), jnp.float32)
        for tap_index in range(TAP_COUNT):
            window = lax.dynamic_slice_in_dim(
                source_sec, source_depth - 1 + tap_index + shift_value, row_count, 0
            )
            running = running + weights[tap_index][:, None] * window.astype(jnp.float32)
        return running.astype(jnp.bfloat16)

    row_warped = jax.vmap(warp_rows)(source, row_weights, row_shift[:, 0])
    row_ids = lax.broadcasted_iota(jnp.int32, (col_count, col_count), 0)
    col_ids = lax.broadcasted_iota(jnp.int32, (col_count, col_count), 1)

    def column_matrix(weights, shift_value):
        offsets = row_ids - col_ids - shift_value + 1
        matrix = jnp.zeros((col_count, col_count), jnp.bfloat16)
        for tap_index in range(TAP_COUNT):
            matrix = jnp.where(offsets == tap_index, weights[tap_index][None, :], matrix)
        return matrix

    matrices = jax.vmap(column_matrix)(col_weights, col_shift)
    warped = jnp.einsum(
        "srw,swv->srv", row_warped, matrices, preferred_element_type=jnp.float32
    ).astype(jnp.bfloat16)
    depth = RADIUS
    rimmed = padded_2(warped, (("strip", 1),), depth)
    hops = (PAIR_REACH + sec_count - 1) // sec_count
    first_global = sec_pos * sec_count
    padded_on = jnp.concatenate([jnp.zeros((PAIR_REACH, PAIR_REACH), jnp.int32), pair_on], 0)
    on_rows = lax.dynamic_slice_in_dim(padded_on, first_global, sec_count + PAIR_REACH, 0).astype(
        jnp.float32
    )
    pieces = {}
    section = 0
    pieces[section] = rimmed[section]
    for hop in range(1, hops + 1):
        arrived = passed_along(rimmed, "sec", -hop)
        slot_pos = 0
        pieces[hop * sec_count + slot_pos] = arrived[slot_pos]
    gradient_sums = {}
    section = 0
    for distance in range(1, PAIR_REACH + 1):
        global_first = first_global + section
        inside = (global_first >= 0) & (global_first + distance < total_sections)
        grad_left, grad_right = pair_grads(
            pieces[section],
            pieces[section + distance],
            on_rows[section + PAIR_REACH, distance - 1] * inside.astype(jnp.float32),
            depth,
            row_count,
        )
        for target, term in ((section, grad_left), (section + distance, grad_right)):
            if target in gradient_sums:
                gradient_sums[target] = gradient_sums[target] + term
            else:
                gradient_sums[target] = term
    section = 0
    own_grads = [gradient_sums[section]]
    for hop in range(1, hops + 1):
        parcel = jnp.stack([gradient_sums[hop * sec_count]])
        returned = passed_along(parcel, "sec", hop)
        slot_pos = 0
        own_grads[slot_pos] = own_grads[slot_pos] + returned[slot_pos]
    grad_warped = jnp.stack(own_grads)
    middle = rimmed[:, depth - 1 : depth + row_count + 1].astype(jnp.float32)
    slope_rows = (middle[:, 2:] - middle[:, :-2]) * 0.5
    centre = middle[:, 1:-1]
    side_padded = jnp.pad(centre, ((0, 0), (0, 0), (1, 1)))
    slope_cols = (side_padded[:, :, 2:] - side_padded[:, :, :-2]) * 0.5
    products = jnp.stack([grad_warped * slope_rows, grad_warped * slope_cols])
    widened = padded_2(products, (("strip", 2),), RADIUS)
    displacement = -box_sum(widened, row_count) / 9.0
    return (grad_warped, displacement)


MESH = pl.DeviceIdType.MESH
BLOCK = 16
HALF_ROWS = BLOCK // 2
LANES = 128
COL_TILE = 256


def rows_sum_from(x):
    m = x.shape[0]
    t = x + pltpu.roll(x, m - 1, 0) + pltpu.roll(x, m - 2, 0)
    t = t + pltpu.roll(t, m - 3, 0) + pltpu.roll(t, m - 6, 0)
    return t[: m - 2 * RADIUS]


def rows_sum_centred(x):
    m = x.shape[0]
    t = x + pltpu.roll(x, m - 1, 0) + pltpu.roll(x, 1, 0)
    return t + pltpu.roll(t, m - 3, 0) + pltpu.roll(t, 3, 0)


def with_zero_lanes(x):
    return jnp.concatenate([x, jnp.zeros((x.shape[0], LANES), x.dtype)], axis=1)


def cols_sum(x):
    width = x.shape[1]
    x = with_zero_lanes(x)
    m = width + LANES
    t = x + pltpu.roll(x, m - 1, 1) + pltpu.roll(x, 1, 1)
    t = t + pltpu.roll(t, m - 3, 1) + pltpu.roll(t, 3, 1)
    return t[:, :width]


def halves_to_rows(x):
    x = x.astype(jnp.float32)
    count, _, half = x.shape
    rows = jnp.concatenate([x[:, :HALF_ROWS], x[:, HALF_ROWS:]], axis=2)
    return rows.reshape(count * HALF_ROWS, 2 * half)


def align_kernel(
    n,
    strips,
    images,
    row_weights,
    row_shift,
    col_weights,
    col_shift,
    pair_on,
    grad_done,
    warp_done,
    grad_ext,
    warp_ext,
    img_ext,
    col_mats,
    window,
    field,
    mean,
    inv,
    ncc_sum,
    mean_sum,
    grad_acc,
    grad_send,
    img_send,
    img_recv,
    halo_send,
    halo_recv,
    win_send,
    win_recv,
    back_send,
    back_recv,
    edge_send,
    edge_recv,
):
    me = lax.axis_index("sec")
    z = lax.axis_index("strip")
    rows, width = images.shape
    f32, bf16 = jnp.float32, jnp.bfloat16
    has_up = z > 0
    has_down = z < strips - 1
    up = {"strip": z - 1}
    down = {"strip": z + 1}
    cells = float((2 * RADIUS + 1) ** 2)


    def remote(src, dst, send, recv, where):
        return pltpu.make_async_remote_copy(
            src_ref=src, dst_ref=dst, send_sem=send, recv_sem=recv, device_id=where, device_id_type=MESH
        )

    barrier = pltpu.get_barrier_semaphore()
    for step in range(1, n):
        pl.semaphore_signal(
            barrier, inc=1, device_id={"sec": lax.rem(me + step, n)}, device_id_type=MESH
        )

    @pl.when(has_up)
    def _():
        pl.semaphore_signal(barrier, inc=1, device_id=up, device_id_type=MESH)

    @pl.when(has_down)
    def _():
        pl.semaphore_signal(barrier, inc=1, device_id=down, device_id_type=MESH)

    pl.semaphore_wait(barrier, n - 1 + jnp.where(has_up, 1, 0) + jnp.where(has_down, 1, 0))

    img_up = remote(
        images.at[pl.ds(0, BLOCK)], img_ext.at[pl.ds(rows + BLOCK, BLOCK)], img_send.at[0], img_recv.at[1], up
    )
    img_down = remote(
        images.at[pl.ds(rows - BLOCK, BLOCK)], img_ext.at[pl.ds(0, BLOCK)], img_send.at[1], img_recv.at[0], down
    )

    def exchange_start(to_up, to_down):
        @pl.when(has_up)
        def _():
            to_up.start()

        @pl.when(has_down)
        def _():
            to_down.start()

    def exchange_wait(to_up, to_down):
        @pl.when(has_up)
        def _():
            to_up.wait_send()
            to_down.wait_recv()

        @pl.when(has_down)
        def _():
            to_down.wait_send()
            to_up.wait_recv()

    exchange_start(img_up, img_down)
    zero_block = jnp.zeros((BLOCK, width), bf16)
    zero_half = jnp.zeros((BLOCK, width // 2), bf16)
    bottom = 2 * n + 1

    @pl.when(jnp.logical_not(has_up))
    def _():
        img_ext[0:BLOCK] = zero_block
        warp_ext[0] = zero_half
        grad_ext[0] = zero_block

    @pl.when(jnp.logical_not(has_down))
    def _():
        img_ext[rows + BLOCK : rows + 2 * BLOCK] = zero_block
        warp_ext[bottom] = zero_half
        grad_ext[n + 1] = zero_block

    col_move = col_shift[0]
    all_taps = col_weights[...].astype(f32)
    spans = []
    tiles = width // COL_TILE
    for tile in range(tiles):
        first = max(0, tile * COL_TILE - LANES)
        last = min(width, (tile + 1) * COL_TILE + LANES)
        spans.append((first, last))
        extent = last - first
        row_ids = lax.broadcasted_iota(jnp.int32, (extent, COL_TILE), 0) + first
        col_ids = lax.broadcasted_iota(jnp.int32, (extent, COL_TILE), 1) + tile * COL_TILE
        offsets = row_ids - col_ids - col_move + 1
        matrix = jnp.zeros((extent, COL_TILE), f32)
        for tap in range(TAP_COUNT):
            taps = all_taps[tap : tap + 1, tile * COL_TILE : (tile + 1) * COL_TILE]
            matrix = jnp.where(offsets == tap, taps, matrix)
        col_mats[tile, 0:extent, :] = matrix.astype(bf16)

    ext = rows + 2 * BLOCK
    source_ids = lax.broadcasted_iota(jnp.int32, (ext, rows), 0)
    target_ids = lax.broadcasted_iota(jnp.int32, (ext, rows), 1)
    offsets = source_ids - target_ids - BLOCK - row_shift[0, 0] + 1
    row_matrix = jnp.zeros((ext, rows), f32)
    for tap in range(TAP_COUNT):
        row_matrix = jnp.where(offsets == tap, row_weights[tap : tap + 1, :], row_matrix)
    parts = []
    rest = row_matrix
    for _ in range(3):
        part = rest.astype(bf16)
        parts.append(part)
        rest = rest - part.astype(f32)

    img_ext[BLOCK : rows + BLOCK] = images[...]
    exchange_wait(img_up, img_down)
    row_warped = jnp.zeros((rows, width), f32)
    for part in reversed(parts):
        row_warped = row_warped + lax.dot_general(
            part, img_ext[...], (((0,), (0,)), ((), ())), preferred_element_type=f32
        )
    row_warped = row_warped.astype(bf16)

    def warped_tile(tile):
        first, last = spans[tile]
        piece = jnp.dot(
            row_warped[:, first:last], col_mats[tile, 0 : last - first, :], preferred_element_type=f32
        )
        return piece.reshape(2 * n, HALF_ROWS, COL_TILE)

    for tile in range(tiles // 2):
        both = jnp.concatenate([warped_tile(tile), warped_tile(tile + tiles // 2)], axis=1)
        warp_ext[1:bottom, :, tile * COL_TILE : (tile + 1) * COL_TILE] = both.astype(bf16)

    halo_up = remote(warp_ext.at[1], warp_ext.at[bottom], halo_send.at[0], halo_recv.at[1], up)
    halo_down = remote(warp_ext.at[bottom - 1], warp_ext.at[0], halo_send.at[1], halo_recv.at[0], down)
    exchange_start(halo_up, halo_down)

    def window_copy(target):
        return remote(
            warp_ext.at[pl.ds(2 * target, 4)], window.at[me], win_send.at[target], win_recv.at[me], {"sec": target}
        )

    def send_inner(step, carry):
        target = lax.rem(me + n - step, n)

        @pl.when((target > 0) & (target < n - 1))
        def _():
            window_copy(target).start()

        return carry

    def send_outer(step, carry):
        target = lax.rem(me + n - step, n)

        @pl.when((target == 0) | (target == n - 1))
        def _():
            window_copy(target).start()

        return carry

    lax.fori_loop(1, n, send_inner, 0)
    exchange_wait(halo_up, halo_down)
    lax.fori_loop(1, n, send_outer, 0)
    window[me] = warp_ext[pl.ds(2 * me, 4)]

    mid_rows = BLOCK + 2 * RADIUS
    row_ids = lax.broadcasted_iota(jnp.int32, (mid_rows, width), 0) + (z * rows + me * BLOCK - RADIUS)
    inside = jnp.where((row_ids >= 0) & (row_ids < strips * rows), 1.0, 0.0).astype(f32)

    def one_pair(left, right, distance):
        weight = pair_on[distance - 1, left].astype(f32)
        a, b = field[left], field[right]
        mean_a, mean_b = mean[left], mean[right]
        cov = cols_sum(rows_sum_from(a * b)) * (1.0 / cells) - mean_a * mean_b
        scale = inv[left] * inv[right] * (inside * weight)
        ncc = cov * scale
        ncc_sum[left] += ncc
        ncc_sum[right] += ncc
        mean_sum[left] += scale * mean_b
        mean_sum[right] += scale * mean_a
        boxed = cols_sum(rows_sum_from(scale))
        grad_acc[left] += boxed * b[HALF_ROWS : HALF_ROWS + BLOCK]
        grad_acc[right] += boxed * a[HALF_ROWS : HALF_ROWS + BLOCK]

    def meet(step, carry):
        sec = lax.rem(me + step, n)

        @pl.when(step > 0)
        def _():
            remote(
                warp_ext.at[pl.ds(0, 4)], window.at[sec], win_send.at[sec], win_recv.at[sec], {"sec": sec}
            ).wait_recv()

        values = halves_to_rows(window[sec])
        field[sec] = values
        average = cols_sum(rows_sum_from(values)) * (1.0 / cells)
        square = cols_sum(rows_sum_from(values * values)) * (1.0 / cells)
        mean[sec] = average
        inv[sec] = lax.rsqrt(square - average * average + variance_bias)
        ncc_sum[sec] = jnp.zeros((mid_rows, width), f32)
        mean_sum[sec] = jnp.zeros((mid_rows, width), f32)
        grad_acc[sec] = jnp.zeros((BLOCK, width), f32)

        def with_earlier(distance, carry):
            @pl.when((sec >= distance) & (lax.rem(sec - distance - me + 2 * n, n) < step))
            def _():
                one_pair(lax.rem(sec - distance + n, n), sec, distance)

            @pl.when((sec + distance < n) & (lax.rem(sec + distance - me + 2 * n, n) < step))
            def _():
                one_pair(sec, lax.rem(sec + distance, n), distance)

            return carry

        lax.fori_loop(1, PAIR_REACH + 1, with_earlier, 0)
        return carry

    lax.fori_loop(0, n, meet, 0)

    def back_copy(sec):
        return remote(
            grad_send.at[sec], grad_ext.at[me + 1], back_send.at[sec], back_recv.at[me], {"sec": sec}
        )

    def finish(step, carry):
        sec = lax.rem(me + 1 + step, n)
        root = inv[sec]
        g_twice = ncc_sum[sec] * root * root
        h = mean_sum[sec] - mean[sec] * g_twice
        boxed_h = cols_sum(rows_sum_from(h))
        boxed_g = cols_sum(rows_sum_from(g_twice))
        mid = field[sec, HALF_ROWS : HALF_ROWS + BLOCK, :]
        total = (boxed_h + mid * boxed_g - grad_acc[sec]) * (1.0 / cells)
        grad_send[sec] = total.astype(bf16)

        @pl.when(sec != me)
        def _():
            back_copy(sec).start()

        return carry

    lax.fori_loop(0, n, finish, 0)
    grad_ext[me + 1] = grad_send[me]

    def drain(step, carry):
        sec = lax.rem(me + step, n)

        @pl.when(step > 0)
        def _():
            window_copy(sec).wait_send()
            back_copy(sec).wait_send()
            remote(
                grad_send.at[sec], grad_ext.at[sec + 1], back_send.at[sec], back_recv.at[sec], {"sec": sec}
            ).wait_recv()

        return carry

    lax.fori_loop(0, n, drain, 0)

    edge_up = remote(grad_ext.at[1], grad_ext.at[n + 1], edge_send.at[0], edge_recv.at[1], up)
    edge_down = remote(grad_ext.at[n], grad_ext.at[0], edge_send.at[1], edge_recv.at[0], down)
    exchange_start(edge_up, edge_down)
    exchange_wait(edge_up, edge_down)
    grad_done[...] = grad_ext[...]
    warp_done[...] = warp_ext[...]


def displace_kernel(n, grad_ext, warp_ext, grad_out, disp_out, grad_rows, disp_rows, terms, sems):
    _, rows, width = grad_rows.shape
    f32, bf16 = jnp.float32, jnp.bfloat16
    grads = grad_ext[...].reshape((n + 2) * BLOCK, width).astype(f32)
    grad_rows[0] = grads[BLOCK : BLOCK + rows]
    grad_copy = pltpu.make_async_copy(grad_rows, grad_out, sems.at[2])
    grad_copy.start()
    near = rows + 2 * HALF_ROWS
    near_grads = grads[HALF_ROWS : HALF_ROWS + near] * (-0.5 / 9.0)
    warped = halves_to_rows(warp_ext[...])
    slope_rows = pltpu.roll(warped, near - 1, 0) - pltpu.roll(warped, 1, 0)
    padded = with_zero_lanes(warped)
    lanes = width + LANES
    slope_cols = (pltpu.roll(padded, lanes - 1, 1) - pltpu.roll(padded, 1, 1))[:, :width]

    out_ids = lax.broadcasted_iota(jnp.int32, (rows, near), 0)
    in_ids = lax.broadcasted_iota(jnp.int32, (rows, near), 1)
    row_band = jnp.where(jnp.abs(in_ids - out_ids - HALF_ROWS) <= RADIUS, 1.0, 0.0).astype(bf16)
    in_ids = lax.broadcasted_iota(jnp.int32, (COL_TILE + 2 * LANES, COL_TILE), 0)
    out_ids = lax.broadcasted_iota(jnp.int32, (COL_TILE + 2 * LANES, COL_TILE), 1)
    col_band = jnp.where(jnp.abs(in_ids - out_ids - LANES) <= RADIUS, 1.0, 0.0).astype(bf16)

    def halves(x):
        top = x.astype(bf16)
        return top, (x - top.astype(f32)).astype(bf16)

    for part, slope in enumerate((slope_rows, slope_cols)):
        top, rest = halves(near_grads * slope)
        summed = jnp.dot(row_band, rest, preferred_element_type=f32)
        summed = summed + jnp.dot(row_band, top, preferred_element_type=f32)
        top, rest = halves(summed)
        terms[0:rows] = top
        terms[rows : 2 * rows] = rest
        for tile in range(width // COL_TILE):
            base = tile * COL_TILE - LANES
            first = max(0, base)
            last = min(width, (tile + 1) * COL_TILE + LANES)
            boxed = jnp.dot(terms[:, first:last], col_band[first - base : last - base], preferred_element_type=f32)
            disp_rows[part, 0, :, tile * COL_TILE : (tile + 1) * COL_TILE] = boxed[:rows] + boxed[rows:]
        pltpu.make_async_copy(disp_rows.at[part], disp_out.at[part], sems.at[part]).start()

    for part in range(2):
        pltpu.make_async_copy(disp_rows.at[part], disp_out.at[part], sems.at[part]).wait()
    grad_copy.wait()


def fused(n, strips, images, row_weights, row_shift, col_weights, col_shift, pair_on):
    _, rows, width = images.shape
    f32, bf16 = jnp.float32, jnp.bfloat16
    mid_rows = BLOCK + 2 * RADIUS
    vmem = pl.BlockSpec(memory_space=pltpu.VMEM)
    smem = pl.BlockSpec(memory_space=pltpu.SMEM)
    where = pl.BlockSpec(memory_space=pltpu.HBM)
    dma = pltpu.SemaphoreType.DMA
    grad_ext, warp_ext = pl.pallas_call(
        functools.partial(align_kernel, n, strips),
        out_shape=(
            jax.ShapeDtypeStruct((n + 2, BLOCK, width), bf16),
            jax.ShapeDtypeStruct((2 * n + 2, BLOCK, width // 2), bf16),
        ),
        in_specs=[vmem, vmem, smem, vmem, smem, smem],
        out_specs=(vmem, vmem),
        scratch_shapes=[
            pltpu.VMEM((n + 2, BLOCK, width), bf16),
            pltpu.VMEM((2 * n + 2, BLOCK, width // 2), bf16),
            pltpu.VMEM((rows + 2 * BLOCK, width), bf16),
            pltpu.VMEM((width // COL_TILE, COL_TILE + 2 * LANES, COL_TILE), bf16),
            pltpu.VMEM((n, 4, BLOCK, width // 2), bf16),
            pltpu.VMEM((n, 2 * BLOCK, width), f32),
            pltpu.VMEM((n, mid_rows, width), f32),
            pltpu.VMEM((n, mid_rows, width), f32),
            pltpu.VMEM((n, mid_rows, width), f32),
            pltpu.VMEM((n, mid_rows, width), f32),
            pltpu.VMEM((n, BLOCK, width), f32),
            pltpu.VMEM((n, BLOCK, width), bf16),
            dma((2,)),
            dma((2,)),
            dma((2,)),
            dma((2,)),
            dma((n,)),
            dma((n,)),
            dma((n,)),
            dma((n,)),
            dma((n,)),
            dma((2,)),
        ],
        compiler_params=pltpu.CompilerParams(
            collective_id=0, has_side_effects=True, vmem_limit_bytes=40 * 1024 * 1024
        ),
    )(images[0], row_weights[0], row_shift, col_weights[0], col_shift, pair_on.T)
    return pl.pallas_call(
        functools.partial(displace_kernel, n),
        out_shape=(
            jax.ShapeDtypeStruct((1, rows, width), f32),
            jax.ShapeDtypeStruct((2, 1, rows, width), f32),
        ),
        in_specs=[vmem, vmem],
        out_specs=(where, where),
        scratch_shapes=[
            pltpu.VMEM((1, rows, width), f32),
            pltpu.VMEM((2, 1, rows, width), f32),
            pltpu.VMEM((2 * rows, width), bf16),
            dma((3,)),
        ],
        compiler_params=pltpu.CompilerParams(vmem_limit_bytes=40 * 1024 * 1024),
    )(grad_ext, warp_ext)


def solution(mesh):
    n, strips = mesh.shape["sec"], mesh.shape["strip"]

    def step(images, *rest):
        sections, rows, width = images.shape
        if sections == 1 and rows == n * BLOCK and width % (2 * COL_TILE) == 0:
            return fused(n, strips, images, *rest)
        return per_device(images, *rest)

    return jax.shard_map(
        step,
        mesh=mesh,
        in_specs=(
            P("sec", "strip", None),
            P("sec", None, "strip"),
            P("sec", "strip"),
            P("sec", None, None),
            P("sec"),
            P(),
        ),
        out_specs=(P("sec", "strip", None), P(None, "sec", "strip", None)),
        check_vma=False,
    )
```

```python
import functools

import jax
import jax.numpy as jnp
from jax import lax
from jax.experimental import pallas as pl
from jax.experimental.pallas import tpu as pltpu
from jax.sharding import PartitionSpec as P

TAP_COUNT = 4
MAX_SHIFT = 4
RADIUS = 4
PAIR_REACH = 3


variance_bias = 0.25


def padded_2(block, sides, width):
    for axis, dim in sides:
        count = lax.axis_size(axis)
        forward = [(i, i + 1) for i in range(count - 1)]
        backward = [(target, source) for source, target in forward]
        low = lax.ppermute(
            lax.slice_in_dim(block, block.shape[dim] - width, None, axis=dim), axis, forward
        )
        high = lax.ppermute(lax.slice_in_dim(block, 0, width, axis=dim), axis, backward)
        block = jnp.concatenate([low, block, high], axis=dim)
    return block


def passed_along(value, axis, steps):
    count = lax.axis_size(axis)
    initial, last = (max(0, -steps), min(count, count - steps))
    return lax.ppermute(value, axis, [(source, source + steps) for source in range(initial, last)])


def box_rows(field, out_rows):
    running = field[..., 0:out_rows, :]
    for step_row in range(1, 2 * RADIUS + 1):
        running = running + field[..., step_row : step_row + out_rows, :]
    return running


def box_cols(field):
    col_count = field.shape[-1]
    widths = [(0, 0)] * (field.ndim - 1) + [(RADIUS, RADIUS)]
    padded = jnp.pad(field, widths)
    running = padded[..., 0:col_count]
    for step_col in range(1, 2 * RADIUS + 1):
        running = running + padded[..., step_col : step_col + col_count]
    return running


def box_sum(field, out_rows):
    return box_cols(box_rows(field, out_rows))


def pair_grads(left_rim, right_rim, weight, depth, row_count):
    box_cells = float((2 * RADIUS + 1) ** 2)
    left_field = left_rim.astype(jnp.float32)
    right_field = right_rim.astype(jnp.float32)
    mean_left = box_sum(left_field, row_count) / box_cells
    mean_right = box_sum(right_field, row_count) / box_cells
    var_left = (
        box_sum(left_field * left_field, row_count) / box_cells
        - mean_left * mean_left
        + variance_bias
    )
    var_right = (
        box_sum(right_field * right_field, row_count) / box_cells
        - mean_right * mean_right
        + variance_bias
    )
    covariance = box_sum(left_field * right_field, row_count) / box_cells - mean_left * mean_right
    denom_root = jnp.sqrt(var_left * var_right)
    ncc_value = covariance / denom_root
    g_cov = -weight / denom_root
    g_left = weight * ncc_value / (2.0 * var_left)
    g_right = weight * ncc_value / (2.0 * var_right)
    h_left = -g_cov * mean_right - 2.0 * g_left * mean_left
    h_right = -g_cov * mean_left - 2.0 * g_right * mean_right
    stacked = jnp.stack([g_cov, g_left, g_right, h_left, h_right])
    widened = padded_2(stacked.astype(jnp.bfloat16), (("strip", 1),), RADIUS).astype(stacked.dtype)
    boxed = box_sum(widened, row_count)
    mid_left = left_field[depth : depth + row_count]
    mid_right = right_field[depth : depth + row_count]
    grad_left = (boxed[3] + 2.0 * mid_left * boxed[1] + mid_right * boxed[0]) / box_cells
    grad_right = (boxed[4] + 2.0 * mid_right * boxed[2] + mid_left * boxed[0]) / box_cells
    return (grad_left, grad_right)


def per_device(images, row_weights, row_shift, col_weights, col_shift, pair_on):
    sec_count, row_count, col_count = images.shape
    sec_pos = lax.axis_index("sec")
    total_sections = sec_count * lax.axis_size("sec")
    source_depth = MAX_SHIFT + 2
    source = padded_2(images, (("strip", 1),), source_depth)

    def warp_rows(source_sec, weights, shift_value):
        running = jnp.zeros((row_count, col_count), jnp.float32)
        for tap_index in range(TAP_COUNT):
            window = lax.dynamic_slice_in_dim(
                source_sec, source_depth - 1 + tap_index + shift_value, row_count, 0
            )
            running = running + weights[tap_index][:, None] * window.astype(jnp.float32)
        return running.astype(jnp.bfloat16)

    row_warped = jax.vmap(warp_rows)(source, row_weights, row_shift[:, 0])
    row_ids = lax.broadcasted_iota(jnp.int32, (col_count, col_count), 0)
    col_ids = lax.broadcasted_iota(jnp.int32, (col_count, col_count), 1)

    def column_matrix(weights, shift_value):
        offsets = row_ids - col_ids - shift_value + 1
        matrix = jnp.zeros((col_count, col_count), jnp.bfloat16)
        for tap_index in range(TAP_COUNT):
            matrix = jnp.where(offsets == tap_index, weights[tap_index][None, :], matrix)
        return matrix

    matrices = jax.vmap(column_matrix)(col_weights, col_shift)
    warped = jnp.einsum(
        "srw,swv->srv", row_warped, matrices, preferred_element_type=jnp.float32
    ).astype(jnp.bfloat16)
    depth = RADIUS
    rimmed = padded_2(warped, (("strip", 1),), depth)
    hops = (PAIR_REACH + sec_count - 1) // sec_count
    first_global = sec_pos * sec_count
    padded_on = jnp.concatenate([jnp.zeros((PAIR_REACH, PAIR_REACH), jnp.int32), pair_on], 0)
    on_rows = lax.dynamic_slice_in_dim(padded_on, first_global, sec_count + PAIR_REACH, 0).astype(
        jnp.float32
    )
    pieces = {}
    section = 0
    pieces[section] = rimmed[section]
    for hop in range(1, hops + 1):
        arrived = passed_along(rimmed, "sec", -hop)
        slot_pos = 0
        pieces[hop * sec_count + slot_pos] = arrived[slot_pos]
    gradient_sums = {}
    section = 0
    for distance in range(1, PAIR_REACH + 1):
        global_first = first_global + section
        inside = (global_first >= 0) & (global_first + distance < total_sections)
        grad_left, grad_right = pair_grads(
            pieces[section],
            pieces[section + distance],
            on_rows[section + PAIR_REACH, distance - 1] * inside.astype(jnp.float32),
            depth,
            row_count,
        )
        for target, term in ((section, grad_left), (section + distance, grad_right)):
            if target in gradient_sums:
                gradient_sums[target] = gradient_sums[target] + term
            else:
                gradient_sums[target] = term
    section = 0
    own_grads = [gradient_sums[section]]
    for hop in range(1, hops + 1):
        parcel = jnp.stack([gradient_sums[hop * sec_count]])
        returned = passed_along(parcel, "sec", hop)
        slot_pos = 0
        own_grads[slot_pos] = own_grads[slot_pos] + returned[slot_pos]
    grad_warped = jnp.stack(own_grads)
    middle = rimmed[:, depth - 1 : depth + row_count + 1].astype(jnp.float32)
    slope_rows = (middle[:, 2:] - middle[:, :-2]) * 0.5
    centre = middle[:, 1:-1]
    side_padded = jnp.pad(centre, ((0, 0), (0, 0), (1, 1)))
    slope_cols = (side_padded[:, :, 2:] - side_padded[:, :, :-2]) * 0.5
    products = jnp.stack([grad_warped * slope_rows, grad_warped * slope_cols])
    widened = padded_2(products, (("strip", 2),), RADIUS)
    displacement = -box_sum(widened, row_count) / 9.0
    return (grad_warped, displacement)


MESH = pl.DeviceIdType.MESH
BLOCK = 16
HALF_ROWS = BLOCK // 2
LANES = 128
COL_TILE = 256


def rows_sum_from(x):
    m = x.shape[0]
    t = x + pltpu.roll(x, m - 1, 0) + pltpu.roll(x, m - 2, 0)
    t = t + pltpu.roll(t, m - 3, 0) + pltpu.roll(t, m - 6, 0)
    return t[: m - 2 * RADIUS]


def rows_sum_centred(x):
    m = x.shape[0]
    t = x + pltpu.roll(x, m - 1, 0) + pltpu.roll(x, 1, 0)
    return t + pltpu.roll(t, m - 3, 0) + pltpu.roll(t, 3, 0)


def with_zero_lanes(x):
    return jnp.concatenate([x, jnp.zeros((x.shape[0], LANES), x.dtype)], axis=1)


def cols_sum(x):
    width = x.shape[1]
    x = with_zero_lanes(x)
    m = width + LANES
    t = x + pltpu.roll(x, m - 1, 1) + pltpu.roll(x, 1, 1)
    t = t + pltpu.roll(t, m - 3, 1) + pltpu.roll(t, 3, 1)
    return t[:, :width]


def halves_to_rows(x):
    x = x.astype(jnp.float32)
    count, _, half = x.shape
    rows = jnp.concatenate([x[:, :HALF_ROWS], x[:, HALF_ROWS:]], axis=2)
    return rows.reshape(count * HALF_ROWS, 2 * half)


def align_kernel(
    n,
    strips,
    images,
    row_weights,
    row_shift,
    col_weights,
    col_shift,
    pair_on,
    grad_done,
    warp_done,
    grad_ext,
    warp_ext,
    img_ext,
    col_mats,
    window,
    field,
    mean,
    inv,
    ncc_sum,
    mean_sum,
    grad_acc,
    grad_send,
    in_sems,
    img_send,
    img_recv,
    halo_send,
    halo_recv,
    win_send,
    win_recv,
    back_send,
    back_recv,
    edge_send,
    edge_recv,
):
    me = lax.axis_index("sec")
    z = lax.axis_index("strip")
    rows, width = images.shape
    f32, bf16 = jnp.float32, jnp.bfloat16
    has_up = z > 0
    has_down = z < strips - 1
    up = {"strip": z - 1}
    down = {"strip": z + 1}
    cells = float((2 * RADIUS + 1) ** 2)


    def remote(src, dst, send, recv, where):
        return pltpu.make_async_remote_copy(
            src_ref=src, dst_ref=dst, send_sem=send, recv_sem=recv, device_id=where, device_id_type=MESH
        )

    own_in = pltpu.make_async_copy(images, img_ext.at[pl.ds(BLOCK, rows)], in_sems.at[0])
    own_in.start()
    barrier = pltpu.get_barrier_semaphore()
    for step in range(1, n):
        pl.semaphore_signal(
            barrier, inc=1, device_id={"sec": lax.rem(me + step, n)}, device_id_type=MESH
        )

    @pl.when(has_up)
    def _():
        pl.semaphore_signal(barrier, inc=1, device_id=up, device_id_type=MESH)

    @pl.when(has_down)
    def _():
        pl.semaphore_signal(barrier, inc=1, device_id=down, device_id_type=MESH)

    pl.semaphore_wait(barrier, n - 1 + jnp.where(has_up, 1, 0) + jnp.where(has_down, 1, 0))

    img_up = remote(
        images.at[pl.ds(0, BLOCK)], img_ext.at[pl.ds(rows + BLOCK, BLOCK)], img_send.at[0], img_recv.at[1], up
    )
    img_down = remote(
        images.at[pl.ds(rows - BLOCK, BLOCK)], img_ext.at[pl.ds(0, BLOCK)], img_send.at[1], img_recv.at[0], down
    )

    def exchange_start(to_up, to_down):
        @pl.when(has_up)
        def _():
            to_up.start()

        @pl.when(has_down)
        def _():
            to_down.start()

    def exchange_wait(to_up, to_down):
        @pl.when(has_up)
        def _():
            to_up.wait_send()
            to_down.wait_recv()

        @pl.when(has_down)
        def _():
            to_down.wait_send()
            to_up.wait_recv()

    exchange_start(img_up, img_down)
    zero_block = jnp.zeros((BLOCK, width), bf16)
    zero_half = jnp.zeros((BLOCK, width // 2), bf16)
    bottom = 2 * n + 1

    @pl.when(jnp.logical_not(has_up))
    def _():
        img_ext[0:BLOCK] = zero_block
        warp_ext[0] = zero_half
        grad_ext[0] = zero_block

    @pl.when(jnp.logical_not(has_down))
    def _():
        img_ext[rows + BLOCK : rows + 2 * BLOCK] = zero_block
        warp_ext[bottom] = zero_half
        grad_ext[n + 1] = zero_block

    col_move = col_shift[0]
    all_taps = col_weights[...].astype(f32)
    spans = []
    tiles = width // COL_TILE
    for tile in range(tiles):
        first = max(0, tile * COL_TILE - LANES)
        last = min(width, (tile + 1) * COL_TILE + LANES)
        spans.append((first, last))
        extent = last - first
        row_ids = lax.broadcasted_iota(jnp.int32, (extent, COL_TILE), 0) + first
        col_ids = lax.broadcasted_iota(jnp.int32, (extent, COL_TILE), 1) + tile * COL_TILE
        offsets = row_ids - col_ids - col_move + 1
        matrix = jnp.zeros((extent, COL_TILE), f32)
        for tap in range(TAP_COUNT):
            taps = all_taps[tap : tap + 1, tile * COL_TILE : (tile + 1) * COL_TILE]
            matrix = jnp.where(offsets == tap, taps, matrix)
        col_mats[tile, 0:extent, :] = matrix.astype(bf16)

    ext = rows + 2 * BLOCK
    source_ids = lax.broadcasted_iota(jnp.int32, (ext, rows), 0)
    target_ids = lax.broadcasted_iota(jnp.int32, (ext, rows), 1)
    offsets = source_ids - target_ids - BLOCK - row_shift[0, 0] + 1
    row_matrix = jnp.zeros((ext, rows), f32)
    for tap in range(TAP_COUNT):
        row_matrix = jnp.where(offsets == tap, row_weights[tap : tap + 1, :], row_matrix)
    parts = []
    rest = row_matrix
    for _ in range(3):
        part = rest.astype(bf16)
        parts.append(part)
        rest = rest - part.astype(f32)

    own_in.wait()
    exchange_wait(img_up, img_down)
    row_warped = jnp.zeros((rows, width), f32)
    for part in reversed(parts):
        row_warped = row_warped + lax.dot_general(
            part, img_ext[...], (((0,), (0,)), ((), ())), preferred_element_type=f32
        )
    row_warped = row_warped.astype(bf16)

    def warped_tile(tile):
        first, last = spans[tile]
        piece = jnp.dot(
            row_warped[:, first:last], col_mats[tile, 0 : last - first, :], preferred_element_type=f32
        )
        return piece.reshape(2 * n, HALF_ROWS, COL_TILE)

    for tile in range(tiles // 2):
        both = jnp.concatenate([warped_tile(tile), warped_tile(tile + tiles // 2)], axis=1)
        warp_ext[1:bottom, :, tile * COL_TILE : (tile + 1) * COL_TILE] = both.astype(bf16)

    halo_up = remote(warp_ext.at[1], warp_ext.at[bottom], halo_send.at[0], halo_recv.at[1], up)
    halo_down = remote(warp_ext.at[bottom - 1], warp_ext.at[0], halo_send.at[1], halo_recv.at[0], down)
    exchange_start(halo_up, halo_down)

    def window_copy(target):
        return remote(
            warp_ext.at[pl.ds(2 * target, 4)], window.at[me], win_send.at[target], win_recv.at[me], {"sec": target}
        )

    def send_inner(step, carry):
        target = lax.rem(me + n - step, n)

        @pl.when((target > 0) & (target < n - 1))
        def _():
            window_copy(target).start()

        return carry

    def send_outer(step, carry):
        target = lax.rem(me + n - step, n)

        @pl.when((target == 0) | (target == n - 1))
        def _():
            window_copy(target).start()

        return carry

    lax.fori_loop(1, n, send_inner, 0)
    exchange_wait(halo_up, halo_down)
    lax.fori_loop(1, n, send_outer, 0)
    window[me] = warp_ext[pl.ds(2 * me, 4)]

    mid_rows = BLOCK + 2 * RADIUS
    row_ids = lax.broadcasted_iota(jnp.int32, (mid_rows, width), 0) + (z * rows + me * BLOCK - RADIUS)
    inside = jnp.where((row_ids >= 0) & (row_ids < strips * rows), 1.0, 0.0).astype(f32)

    def one_pair(left, right, distance):
        weight = pair_on[distance - 1, left].astype(f32)
        a, b = field[left], field[right]
        mean_a, mean_b = mean[left], mean[right]
        cov = cols_sum(rows_sum_from(a * b)) * (1.0 / cells) - mean_a * mean_b
        scale = inv[left] * inv[right] * (inside * weight)
        ncc = cov * scale
        ncc_sum[left] += ncc
        ncc_sum[right] += ncc
        mean_sum[left] += scale * mean_b
        mean_sum[right] += scale * mean_a
        boxed = cols_sum(rows_sum_from(scale))
        grad_acc[left] += boxed * b[HALF_ROWS : HALF_ROWS + BLOCK]
        grad_acc[right] += boxed * a[HALF_ROWS : HALF_ROWS + BLOCK]

    def meet(step, carry):
        sec = lax.rem(me + step, n)

        @pl.when(step > 0)
        def _():
            remote(
                warp_ext.at[pl.ds(0, 4)], window.at[sec], win_send.at[sec], win_recv.at[sec], {"sec": sec}
            ).wait_recv()

        values = halves_to_rows(window[sec])
        field[sec] = values
        average = cols_sum(rows_sum_from(values)) * (1.0 / cells)
        square = cols_sum(rows_sum_from(values * values)) * (1.0 / cells)
        mean[sec] = average
        inv[sec] = lax.rsqrt(square - average * average + variance_bias)
        ncc_sum[sec] = jnp.zeros((mid_rows, width), f32)
        mean_sum[sec] = jnp.zeros((mid_rows, width), f32)
        grad_acc[sec] = jnp.zeros((BLOCK, width), f32)

        def with_earlier(distance, carry):
            @pl.when((sec >= distance) & (lax.rem(sec - distance - me + 2 * n, n) < step))
            def _():
                one_pair(lax.rem(sec - distance + n, n), sec, distance)

            @pl.when((sec + distance < n) & (lax.rem(sec + distance - me + 2 * n, n) < step))
            def _():
                one_pair(sec, lax.rem(sec + distance, n), distance)

            return carry

        lax.fori_loop(1, PAIR_REACH + 1, with_earlier, 0)
        return carry

    lax.fori_loop(0, n, meet, 0)

    def back_copy(sec):
        return remote(
            grad_send.at[sec], grad_ext.at[me + 1], back_send.at[sec], back_recv.at[me], {"sec": sec}
        )

    def finish(step, carry):
        sec = lax.rem(me + 1 + step, n)
        root = inv[sec]
        g_twice = ncc_sum[sec] * root * root
        h = mean_sum[sec] - mean[sec] * g_twice
        boxed_h = cols_sum(rows_sum_from(h))
        boxed_g = cols_sum(rows_sum_from(g_twice))
        mid = field[sec, HALF_ROWS : HALF_ROWS + BLOCK, :]
        total = (boxed_h + mid * boxed_g - grad_acc[sec]) * (1.0 / cells)
        grad_send[sec] = total.astype(bf16)

        @pl.when(sec != me)
        def _():
            back_copy(sec).start()

        return carry

    lax.fori_loop(0, n, finish, 0)
    grad_ext[me + 1] = grad_send[me]

    def take_back(sec):
        remote(
            grad_send.at[sec], grad_ext.at[sec + 1], back_send.at[sec], back_recv.at[sec], {"sec": sec}
        ).wait_recv()

    for sec in (0, n - 1):

        @pl.when(me != sec)
        def _():
            take_back(sec)

    edge_up = remote(grad_ext.at[1], grad_ext.at[n + 1], edge_send.at[0], edge_recv.at[1], up)
    edge_down = remote(grad_ext.at[n], grad_ext.at[0], edge_send.at[1], edge_recv.at[0], down)
    exchange_start(edge_up, edge_down)

    def drain(step, carry):
        sec = lax.rem(me + step, n)
        window_copy(sec).wait_send()
        back_copy(sec).wait_send()

        @pl.when((sec > 0) & (sec < n - 1))
        def _():
            take_back(sec)

        return carry

    lax.fori_loop(1, n, drain, 0)
    exchange_wait(edge_up, edge_down)
    grad_done[...] = grad_ext[...]
    warp_done[...] = warp_ext[...]


def displace_kernel(n, grad_ext, warp_ext, grad_out, disp_out, grad_rows, disp_rows, terms, sems):
    _, rows, width = grad_rows.shape
    f32, bf16 = jnp.float32, jnp.bfloat16
    grads = grad_ext[...].reshape((n + 2) * BLOCK, width).astype(f32)
    grad_rows[0] = grads[BLOCK : BLOCK + rows]
    grad_copy = pltpu.make_async_copy(grad_rows, grad_out, sems.at[2])
    grad_copy.start()
    near = rows + 2 * HALF_ROWS
    near_grads = grads[HALF_ROWS : HALF_ROWS + near] * (-0.5 / 9.0)
    warped = halves_to_rows(warp_ext[...])
    slope_rows = pltpu.roll(warped, near - 1, 0) - pltpu.roll(warped, 1, 0)
    padded = with_zero_lanes(warped)
    lanes = width + LANES
    slope_cols = (pltpu.roll(padded, lanes - 1, 1) - pltpu.roll(padded, 1, 1))[:, :width]

    out_ids = lax.broadcasted_iota(jnp.int32, (rows, near), 0)
    in_ids = lax.broadcasted_iota(jnp.int32, (rows, near), 1)
    row_band = jnp.where(jnp.abs(in_ids - out_ids - HALF_ROWS) <= RADIUS, 1.0, 0.0).astype(bf16)
    in_ids = lax.broadcasted_iota(jnp.int32, (COL_TILE + 2 * LANES, COL_TILE), 0)
    out_ids = lax.broadcasted_iota(jnp.int32, (COL_TILE + 2 * LANES, COL_TILE), 1)
    col_band = jnp.where(jnp.abs(in_ids - out_ids - LANES) <= RADIUS, 1.0, 0.0).astype(bf16)

    def halves(x):
        top = x.astype(bf16)
        return top, (x - top.astype(f32)).astype(bf16)

    for part, slope in enumerate((slope_rows, slope_cols)):
        top, rest = halves(near_grads * slope)
        summed = jnp.dot(row_band, rest, preferred_element_type=f32)
        summed = summed + jnp.dot(row_band, top, preferred_element_type=f32)
        top, rest = halves(summed)
        terms[0:rows] = top
        terms[rows : 2 * rows] = rest
        for tile in range(width // COL_TILE):
            base = tile * COL_TILE - LANES
            first = max(0, base)
            last = min(width, (tile + 1) * COL_TILE + LANES)
            boxed = jnp.dot(terms[:, first:last], col_band[first - base : last - base], preferred_element_type=f32)
            disp_rows[part, 0, :, tile * COL_TILE : (tile + 1) * COL_TILE] = boxed[:rows] + boxed[rows:]
        pltpu.make_async_copy(disp_rows.at[part], disp_out.at[part], sems.at[part]).start()

    for part in range(2):
        pltpu.make_async_copy(disp_rows.at[part], disp_out.at[part], sems.at[part]).wait()
    grad_copy.wait()


def fused(n, strips, images, row_weights, row_shift, col_weights, col_shift, pair_on):
    _, rows, width = images.shape
    f32, bf16 = jnp.float32, jnp.bfloat16
    mid_rows = BLOCK + 2 * RADIUS
    vmem = pl.BlockSpec(memory_space=pltpu.VMEM)
    smem = pl.BlockSpec(memory_space=pltpu.SMEM)
    where = pl.BlockSpec(memory_space=pltpu.HBM)
    dma = pltpu.SemaphoreType.DMA
    grad_ext, warp_ext = pl.pallas_call(
        functools.partial(align_kernel, n, strips),
        out_shape=(
            jax.ShapeDtypeStruct((n + 2, BLOCK, width), bf16),
            jax.ShapeDtypeStruct((2 * n + 2, BLOCK, width // 2), bf16),
        ),
        in_specs=[where, vmem, smem, vmem, smem, smem],
        out_specs=(vmem, vmem),
        scratch_shapes=[
            pltpu.VMEM((n + 2, BLOCK, width), bf16),
            pltpu.VMEM((2 * n + 2, BLOCK, width // 2), bf16),
            pltpu.VMEM((rows + 2 * BLOCK, width), bf16),
            pltpu.VMEM((width // COL_TILE, COL_TILE + 2 * LANES, COL_TILE), bf16),
            pltpu.VMEM((n, 4, BLOCK, width // 2), bf16),
            pltpu.VMEM((n, 2 * BLOCK, width), f32),
            pltpu.VMEM((n, mid_rows, width), f32),
            pltpu.VMEM((n, mid_rows, width), f32),
            pltpu.VMEM((n, mid_rows, width), f32),
            pltpu.VMEM((n, mid_rows, width), f32),
            pltpu.VMEM((n, BLOCK, width), f32),
            pltpu.VMEM((n, BLOCK, width), bf16),
            dma((1,)),
            dma((2,)),
            dma((2,)),
            dma((2,)),
            dma((2,)),
            dma((n,)),
            dma((n,)),
            dma((n,)),
            dma((n,)),
            dma((n,)),
            dma((2,)),
        ],
        compiler_params=pltpu.CompilerParams(
            collective_id=0, has_side_effects=True, vmem_limit_bytes=61500 * 1024
        ),
    )(images[0], row_weights[0], row_shift, col_weights[0], col_shift, pair_on.T)
    return pl.pallas_call(
        functools.partial(displace_kernel, n),
        out_shape=(
            jax.ShapeDtypeStruct((1, rows, width), f32),
            jax.ShapeDtypeStruct((2, 1, rows, width), f32),
        ),
        in_specs=[vmem, vmem],
        out_specs=(where, where),
        scratch_shapes=[
            pltpu.VMEM((1, rows, width), f32),
            pltpu.VMEM((2, 1, rows, width), f32),
            pltpu.VMEM((2 * rows, width), bf16),
            dma((3,)),
        ],
        compiler_params=pltpu.CompilerParams(vmem_limit_bytes=61500 * 1024),
    )(grad_ext, warp_ext)


def solution(mesh):
    n, strips = mesh.shape["sec"], mesh.shape["strip"]

    def step(images, *rest):
        sections, rows, width = images.shape
        if sections == 1 and rows == n * BLOCK and width % (2 * COL_TILE) == 0:
            return fused(n, strips, images, *rest)
        return per_device(images, *rest)

    return jax.shard_map(
        step,
        mesh=mesh,
        in_specs=(
            P("sec", "strip", None),
            P("sec", None, "strip"),
            P("sec", "strip"),
            P("sec", None, None),
            P("sec"),
            P(),
        ),
        out_specs=(P("sec", "strip", None), P(None, "sec", "strip", None)),
        check_vma=False,
    )
```
